32 devices in a mesh: rep: 2 (over x), batch: 16 (over z, y, core).
Axes of the slice: x: 2, y: 2, z: 4, core: 2. Of those that a mesh axis runs over, the one named last changes fastest.
Arguments:
- tokens: bfloat16 [8192, 8192], P(('rep', 'batch')), parts along dimension 0, may hold values from -6 to 6
- key_matrix: bfloat16 [8192, 768], P('batch'), may hold values from -0.0625 to 0.0625
- adapter_down_factors: bfloat16 [8192, 16, 64], P('batch'), may hold values from -0.0625 to 0.0625
- adapter_up_factors: bfloat16 [16, 64, 768], replicated, may hold values from -0.75 to 0.75
- request_block_list: int32 [16], P('rep'), parts along dimension 0, may hold values from 1 to 16, 32 in all
- request_adapter_index: int32 [16], P('rep'), parts along dimension 0, may hold values from 0 to 15
- request_tail_tokens: int32 [16], P('rep'), parts along dimension 0, may hold values from 1 to 128
Outputs:
- keys: bfloat16 [8192, 768], P(('rep', 'batch')), parts along dimension 0
The draws below stay inside these ranges and needn't reach their ends.
There are 2 independent parts, one for each index of `rep`. The reference program is written for one: setup_inputs(seed, part) draws one part's arguments, and reference() takes and returns one part's arrays. A program takes and returns all parts, laid end to end along the dimension named above; an argument that names none is the same for every part. Nothing has to cross between parts.
Inputs may be any that keep to these rules, and one draw needn't show every extreme that they name: request_block_list sum to 32, each at least 1, one exactly 16.
All inputs are finite; a program needn't handle non-finite values.
Results may differ from the reference program's by a relative error of at most 0.004.
Values may be sent and summed in bfloat16 or wider, within the bound.
No kernel may reach another device: no remote copies, remote signals or barrier semaphores. Data moves between devices by JAX's collectives and lax.ppermute only.
A program may use at most 128 MiB of HBM per device.

```python
import math
import jax
import jax.numpy as jnp
import numpy as np
from jax import lax

MODEL_WIDTH = 8192
ADAPTER_RANK = 64
ADAPTER_COUNT = 16
BLOCK = 128
MOST = 16
KEY_FEATURES = 768
TOKENS = 4096
BLOCKS = 32
REQUESTS = 8


def set_ends(entries, rng, smallest, high):
    place = [jax.random.randint(jax.random.fold_in(rng, axis), (), 0, length) for axis, length in enumerate(entries.shape)]
    main_axis = entries.shape.index(max(entries.shape))
    beside = place[:main_axis] + [(place[main_axis] + 1) % entries.shape[main_axis]] + place[main_axis + 1:]
    return entries.at[tuple(place)].set(smallest).at[tuple(beside)].set(high)


def levels(own_key, dims, cuts, least, top_value):
    factor_of, own = 1.0, jax.random.fold_in(own_key, 6)
    for dim, shards_of in cuts:
        heights = jnp.exp(jax.random.uniform(jax.random.fold_in(own, dim), (shards_of,), jnp.float32, least / len(cuts), top_value / len(cuts)))
        factor_of = factor_of * jnp.repeat(heights, dims[dim] // shards_of).reshape([-1 if axis == dim else 1 for axis in range(len(dims))])
    return factor_of


def split_up(number_of, total, bound, lean):
    weights = [(1 << 20) // math.isqrt(rank ** lean) + 1 for rank in range(2, number_of + 1)]
    spare, given = total - bound - (number_of - 1), [1] * (number_of - 1)
    while spare > 0:
        movable = [i for i in range(number_of - 1) if given[i] < bound]
        mass, budget = sum([weights[i] for i in movable]), spare
        for i in movable:
            extra = min(bound - given[i], max(1, budget * weights[i] // mass), spare)
            given[i] = given[i] + extra
            spare = spare - extra
    return np.array([bound] + given)


def uneven(own_key, count, total, most, lean):
    if count == 2:
        one = jax.random.randint(own_key, (), max(1, total - most), min(most, total - 1) + 1)
        return jnp.stack([one, total - one])
    sizes = jnp.asarray(split_up(count, total, most, lean), jnp.int32)
    pairs = (count - 1) // 2
    source_of, taker = sizes[1:1 + 2 * pairs:2], sizes[2:2 + 2 * pairs:2]
    slack = jnp.minimum(source_of - 1, most - taker)
    moved = jax.random.randint(jax.random.fold_in(own_key, 1), (pairs,), 0, 1 << 20) % (slack + 1)
    sizes = sizes.at[1:1 + 2 * pairs:2].set(source_of - moved).at[2:2 + 2 * pairs:2].set(taker + moved)
    return sizes[jax.random.permutation(jax.random.fold_in(own_key, 2), count)]


def bell_draw(rng, shape, deviation, limit, cuts=(), kind=jnp.bfloat16):
    drawn = jax.random.normal(rng, shape, jnp.float32) * deviation
    if len(cuts) > 0:
        drawn = levels(rng, shape, cuts, -0.22, 0.18) * drawn
    return jnp.clip(drawn, min=-limit, max=limit).astype(kind)


def setup_inputs(seed: int = 0, part: int = 0) -> dict:
    seeds = jax.random.split(jax.random.key(seed), 8)
    part_keys = jax.random.split(jax.random.fold_in(seeds[7], part), 8)
    return {
        "tokens": bell_draw(part_keys[0], (TOKENS, MODEL_WIDTH), 1.0, 6.0, ((0, 16),)),
        "key_matrix": bell_draw(seeds[1], (MODEL_WIDTH, KEY_FEATURES), MODEL_WIDTH ** -0.5, 0.0625, ((0, 16),)),
        "adapter_down_factors": bell_draw(seeds[2], (MODEL_WIDTH, ADAPTER_COUNT, ADAPTER_RANK), MODEL_WIDTH ** -0.5, 0.0625, ((0, 16),)),
        "adapter_up_factors": bell_draw(seeds[3], (ADAPTER_COUNT, ADAPTER_RANK, KEY_FEATURES), ADAPTER_RANK ** -0.5, 0.75),
        "request_block_list": uneven(part_keys[4], REQUESTS, BLOCKS, MOST, 2).astype(jnp.int32),
        "request_adapter_index": set_ends(jax.random.randint(part_keys[5], (REQUESTS,), 0, ADAPTER_COUNT), jax.random.fold_in(part_keys[5], 1), 0, ADAPTER_COUNT - 1).astype(jnp.int32),
        "request_tail_tokens": set_ends(jax.random.randint(part_keys[6], (REQUESTS,), 1, BLOCK + 1), jax.random.fold_in(part_keys[6], 1), 1, BLOCK).astype(jnp.int32),
    }


def block_table(request_block_list, request_adapter_index, request_tail_tokens, count_blocks):
    block_ends = jnp.cumsum(request_block_list).astype(jnp.int32)
    block_index = jnp.arange(count_blocks, dtype=jnp.int32)
    owner_req = jnp.sum((block_ends[None, :] <= block_index[:, None]).astype(jnp.int32), axis=1)
    request_ids = jnp.arange(request_block_list.shape[0], dtype=jnp.int32)
    matched = owner_req[:, None] == request_ids[None, :]
    adapter_of = jnp.sum(jnp.where(matched, request_adapter_index[None, :], 0), axis=1).astype(jnp.int32)
    last_of = jnp.sum(jnp.where(matched, block_ends[None, :] - 1, 0), axis=1)
    tail_of = jnp.sum(jnp.where(matched, request_tail_tokens[None, :], 0), axis=1)
    limit_of = jnp.where(last_of == block_index, tail_of, BLOCK).astype(jnp.int32)
    return adapter_of, limit_of


def reference(tokens, key_matrix, adapter_down_factors, adapter_up_factors, request_block_list, request_adapter_index, request_tail_tokens):
    adapter_of, limit_of = block_table(request_block_list, request_adapter_index, request_tail_tokens, BLOCKS)
    base = jnp.dot(tokens, key_matrix, preferred_element_type=jnp.float32)
    blocked = tokens.reshape(BLOCKS, BLOCK, MODEL_WIDTH)

    def one_block(inputs):
        rows_here, picked_index = inputs
        down_selected = jnp.take(adapter_down_factors, picked_index, axis=1)
        up_selected = jnp.take(adapter_up_factors, picked_index, axis=0)
        low = jnp.dot(rows_here, down_selected, preferred_element_type=jnp.float32).astype(jnp.bfloat16)
        return jnp.dot(low, up_selected, preferred_element_type=jnp.float32)

    delta = lax.map(one_block, (blocked, adapter_of))
    live = (jnp.arange(BLOCK, dtype=jnp.int32)[None, :] < limit_of[:, None]).astype(jnp.float32)
    summed = (base.reshape(BLOCKS, BLOCK, KEY_FEATURES) + delta) * live[:, :, None]
    return summed.reshape(TOKENS, KEY_FEATURES).astype(jnp.bfloat16)
```

```python
import jax
import jax.numpy as jnp
from jax import lax
from jax.sharding import PartitionSpec as P

BLOCK = 128
LAYER_CHIPS = 4


def block_table(request_block_list, request_adapter_index, request_tail_tokens, count_blocks):
    block_ends = jnp.cumsum(request_block_list)
    block_index = jnp.arange(count_blocks, dtype=jnp.int32)
    owner_req = jnp.sum((block_ends[None, :] <= block_index[:, None]).astype(jnp.int32), axis=1)
    request_ids = jnp.arange(request_block_list.shape[0], dtype=jnp.int32)
    matched = owner_req[:, None] == request_ids[None, :]
    adapter_of = jnp.sum(jnp.where(matched, request_adapter_index[None, :], 0), axis=1)
    last_of = jnp.sum(jnp.where(matched, block_ends[None, :] - 1, 0), axis=1)
    tail_of = jnp.sum(jnp.where(matched, request_tail_tokens[None, :], 0), axis=1)
    limit_of = jnp.where(last_of == block_index, tail_of, BLOCK)
    return (owner_req, adapter_of, limit_of)


def swap(value, axis, bit):
    return lax.ppermute(value, axis, [(i, i ^ bit) for i in range(lax.axis_size(axis))])


def shards(
    tokens,
    key_matrix,
    adapter_down_factors,
    adapter_up_factors,
    request_block_list,
    request_adapter_index,
    request_tail_tokens,
):
    rows, width = tokens.shape
    depth, out_width = key_matrix.shape
    adapters, rank = adapter_down_factors.shape[1:]
    reps, devices = lax.axis_size("rep"), lax.axis_size("batch")
    group = 2 * LAYER_CHIPS // reps
    layers = devices // group
    part = depth // reps
    rep, me = lax.axis_index("rep"), lax.axis_index("batch")
    layer, spot = me // group, me % group
    local_blocks = rows // BLOCK

    owner_of, adapter_of, limit_of = block_table(
        request_block_list, request_adapter_index, request_tail_tokens, local_blocks * devices
    )

    part_starts = [(rep ^ h) * part for h in range(reps)]

    down = jnp.transpose(adapter_down_factors, (1, 2, 0))
    requests = request_adapter_index.shape[0]
    if requests < adapters:
        slots, slot_of = requests, owner_of
        picks = [request_adapter_index[q] for q in range(requests)]
    else:
        slots, slot_of = adapters, adapter_of
        picks = range(adapters)
    down = jnp.concatenate(
        [
            jnp.concatenate(
                [lax.dynamic_slice(down, (q, 0, start), (1, rank, part)) for q in picks], 0
            )
            for start in part_starts
        ],
        2,
    ).reshape(slots * rank, depth)

    key_parts = [lax.dynamic_slice_in_dim(key_matrix, start, part, 0) for start in part_starts]
    held_key = key_parts[0]
    bundles = []
    bit = layers // 2
    while bit:
        moved = [([bit], swap(held_key, "batch", bit * group), swap(down, "batch", bit * group))]
        if bundles:
            from_keys = [k for _, k, _ in bundles]
            from_downs = [d for _, _, d in bundles]
            from_keys = from_keys[0] if len(bundles) == 1 else jnp.concatenate(from_keys, 0)
            from_downs = from_downs[0] if len(bundles) == 1 else jnp.concatenate(from_downs, 0)
            order = [t ^ bit for ts, _, _ in bundles for t in ts]
            moved.append(
                (order, swap(from_keys, "batch", bit * group), swap(from_downs, "batch", bit * group))
            )
        bundles = bundles + moved
        bit //= 2
    weights, downs = {0: jnp.concatenate(key_parts, 0)}, {0: down}
    for ts, k, d in bundles:
        halves = [k] + [swap(k, "rep", h) for h in range(1, reps)]
        for i, t in enumerate(ts):
            weights[t] = jnp.concatenate([half[i * part : (i + 1) * part] for half in halves], 0)
            downs[t] = d[i * slots * rank : (i + 1) * slots * rank]

    def columns(spot_of, t):
        start = ((layer ^ t) * group + spot_of) * depth
        return [lax.dynamic_slice_in_dim(tokens, start + p, part, 1) for p in part_starts]

    pieces = []
    for s in range(group):
        piece = jnp.concatenate(sum([columns(spot ^ s, t) for t in range(layers)], []), 1)
        pieces.append(swap(piece, "batch", s) if s else piece)
    held = jnp.concatenate(pieces, 0)

    base = low = 0.0
    for t in weights:
        mine = held[:, t * depth : (t + 1) * depth]
        base = base + jnp.dot(mine, weights[t], preferred_element_type=jnp.float32)
        low = low + lax.dot_general(
            mine, downs[t], (((1,), (1,)), ((), ())), preferred_element_type=jnp.float32
        )
    base = base.reshape(group, rows, out_width)

    spots = spot ^ jnp.arange(group, dtype=jnp.int32)
    blocks_of = (layer * group + spots)[:, None] * local_blocks + jnp.arange(local_blocks)[None, :]
    slot_here = jnp.take(slot_of, blocks_of)
    chosen = slot_here[:, :, None] == jnp.arange(slots)[None, None, :]
    low = low.reshape(group, local_blocks, BLOCK, slots, rank)
    low = jnp.sum(jnp.where(chosen[:, :, None, :, None], low, 0.0), axis=3)
    low = low.reshape(group, rows, rank)

    bit = 1
    while bit < group:
        gone = swap(low[1::2], "batch", bit)
        low = low[0::2] + gone
        sent = base[1::2]
        if bit > 1:
            sent = sent.astype(jnp.bfloat16)
        base = base[0::2] + swap(sent, "batch", bit).astype(jnp.float32)
        bit *= 2
    base, low = base[0], low[0].astype(jnp.bfloat16)

    first = me * local_blocks
    my_adapter = lax.dynamic_slice_in_dim(adapter_of, first, local_blocks)
    my_limit = lax.dynamic_slice_in_dim(limit_of, first, local_blocks)
    up = jnp.take(adapter_up_factors, my_adapter, axis=0)
    delta = jnp.einsum(
        "btr,bro->bto", low.reshape(local_blocks, BLOCK, rank), up, preferred_element_type=jnp.float32
    )
    live = (jnp.arange(BLOCK, dtype=jnp.int32)[None, :] < my_limit[:, None]).astype(jnp.float32)
    summed = (base.reshape(local_blocks, BLOCK, out_width) + delta) * live[:, :, None]
    return summed.reshape(rows, out_width).astype(jnp.bfloat16)


def solution(mesh):
    placed = (
        P(("rep", "batch"), None),
        P("batch", None),
        P("batch", None, None),
        P(),
        P("rep"),
        P("rep"),
        P("rep"),
    )
    return jax.shard_map(
        shards, mesh=mesh, in_specs=placed, out_specs=P(("rep", "batch"), None), check_vma=False
    )
```

```python
import functools

import jax
import jax.numpy as jnp
from jax import lax
from jax.experimental import pallas as pl
from jax.experimental.pallas import tpu as pltpu
from jax.sharding import PartitionSpec as P

BLOCK = 128
LANES = 128
LAYER_CHIPS = 4
VMEM_BYTES = 28 * 1024 * 1024

HBM = pl.BlockSpec(memory_space=pl.ANY)
VMEM = pl.BlockSpec(memory_space=pltpu.VMEM)
SMEM = pl.BlockSpec(memory_space=pltpu.SMEM)


def call(kernel, outs, out_specs, in_specs, scratch, flops, moved):
    return pl.pallas_call(
        kernel,
        out_shape=outs,
        in_specs=in_specs,
        out_specs=out_specs,
        scratch_shapes=scratch,
        compiler_params=pltpu.CompilerParams(vmem_limit_bytes=VMEM_BYTES),
        cost_estimate=pl.CostEstimate(flops=flops, bytes_accessed=moved, transcendentals=0),
    )


def swap(value, axis, bit):
    return lax.ppermute(value, axis, [(i, i ^ bit) for i in range(lax.axis_size(axis))])


def run_copies(pairs, sems):
    copies = [pltpu.make_async_copy(a, b, sems.at[i]) for i, (a, b) in enumerate(pairs)]
    for copy in copies:
        copy.start()
    return copies


def part_start(h, part):
    return pl.multiple_of((lax.axis_index("rep") ^ h) * part, part)


def key_parts_kernel(splits, part, key, *refs):
    outs, sems = refs[:splits], refs[splits]
    pairs = [(key.at[pl.ds(part_start(h, part), part), :], outs[h]) for h in range(splits)]
    for copy in run_copies(pairs, sems):
        copy.wait()


def token_pieces_kernel(group, layers, splits, part, tokens, *refs):
    outs, sems = refs[:group], refs[group]
    depth = splits * part
    me = lax.axis_index("batch")
    layer, spot = me // group, me % group
    pairs = []
    for s in reversed(range(group)):
        for t in range(layers):
            first = ((layer ^ t) * group + (spot ^ s)) * depth
            for h in range(splits):
                start = first + part_start(h, part) if splits > 1 else first
                start = pl.multiple_of(start, part)
                pairs.append(
                    (
                        tokens.at[:, pl.ds(start, part)],
                        outs[s].at[:, pl.ds(t * depth + h * part, part)],
                    )
                )
    for copy in run_copies(pairs, sems):
        copy.wait()


def chosen_kernel(slots, rank, splits, part, picks, down, out, sems):
    pairs = []
    for q in range(slots):
        for h in range(splits):
            start = part_start(h, part) if splits > 1 else 0
            pairs.append(
                (
                    down.at[picks[q], :, pl.ds(start, part)],
                    out.at[pl.ds(q * rank, rank), pl.ds(h * part, part)],
                )
            )
    for copy in run_copies(pairs, sems):
        copy.wait()


def base_kernel(rows, depth, layers, entries, count, *refs):
    toks, arrays = refs[:2], refs[2 : 2 + count]
    outs = refs[2 + count : 4 + count]
    held = refs[4 + count]
    weights = refs[5 + count : 5 + 2 * count]
    tok_sems, sems = refs[5 + 2 * count :]
    order = []
    for t, _, _, _, _ in entries:
        if t not in order:
            order.append(t)
    token_copies = {}
    started = {}
    for t in order:
        token_copies[t] = []
        for i in range(2):
            columns = pl.ds(t * depth, depth)
            token_copies[t].append(
                pltpu.make_async_copy(
                    toks[i].at[:, columns], held.at[pl.ds(i * rows, rows), columns], tok_sems.at[i, t]
                )
            )
        for copy in token_copies[t]:
            copy.start()
        for u, a, _, _, _ in entries:
            if u == t and a not in started:
                started[a] = pltpu.make_async_copy(arrays[a], weights[a], sems.at[a])
                started[a].start()
    ready = set()
    for t in order:
        for copy in token_copies[t]:
            copy.wait()
        total = None
        for u, a, row, deep, column in entries:
            if u != t:
                continue
            if a not in ready:
                started[a].wait()
                ready.add(a)
            term = jnp.dot(
                held[:, column : column + deep],
                weights[a][row : row + deep, :],
                preferred_element_type=jnp.float32,
            )
            total = term if total is None else total + term
        for i in range(2):
            here = total[i * rows : (i + 1) * rows]
            if t == order[0]:
                outs[i][...] = here
            else:
                outs[i][...] += here


def table(lists, block):
    sizes, adapters, tails = lists
    end = jnp.int32(0)
    owner, adapter, limit = jnp.int32(0), jnp.int32(0), jnp.int32(BLOCK)
    for q in range(sizes.shape[0]):
        begin = end
        end = end + sizes[q]
        inside = (begin <= block) & (block < end)
        owner = jnp.where(inside, q, owner)
        adapter = jnp.where(inside, adapters[q], adapter)
        limit = jnp.where(inside & (block == end - 1), tails[q], limit)
    return owner, adapter, limit


def low_kernel(
    group, rows, depth, rank, entries, count, by_request, has_sum, last, *refs
):
    lists, refs = refs[:3], refs[3:]
    toks, refs = refs[:group], refs[group:]
    arrays, refs = refs[:count], refs[count:]
    if has_sum:
        before, refs = refs[0], refs[1:]
    if last:
        even, odd, refs = refs[0], refs[1], refs[2:]
    else:
        after, refs = refs[0], refs[1:]
    held, refs = refs[0], refs[1:]
    downs, refs = refs[:count], refs[count:]
    tok_sems, sems = refs
    local_blocks = rows // BLOCK
    me = lax.axis_index("batch")
    layer, spot = me // group, me % group
    first = {}
    started = {}
    for n, (t, a, _) in enumerate(entries):
        if a not in started:
            started[a] = pltpu.make_async_copy(arrays[a], downs[a], sems.at[a])
            started[a].start()
        first[t] = []
        for s in range(group):
            copy = pltpu.make_async_copy(
                toks[s].at[:, pl.ds(t * depth, depth)],
                held.at[pl.ds(s * rows, rows), pl.ds(n * depth, depth)],
                tok_sems.at[s, n],
            )
            copy.start()
            first[t].append(copy)
    slots = []
    for s in range(group):
        for j in range(local_blocks):
            block = (layer * group + (spot ^ s)) * local_blocks + j
            owner, adapter, _ = table(lists, block)
            slots.append(owner if by_request else adapter)
    ready = set()
    wide = 2 * local_blocks
    sums = [before[p] if has_sum else None for p in range(group // 2)]
    for n, (t, a, row) in enumerate(entries):
        for copy in first[t]:
            copy.wait()
        if a not in ready:
            started[a].wait()
            ready.add(a)
        for p in range(group // 2):
            chosen = jnp.concatenate(
                [
                    downs[a][pl.ds(pl.multiple_of(row + slots[p * wide + i] * rank, rank), rank), :]
                    for i in range(wide)
                ],
                0,
            )
            term = lax.dot_general(
                held[2 * p * rows : 2 * (p + 1) * rows, n * depth : (n + 1) * depth],
                chosen,
                (((1,), (1,)), ((), ())),
                preferred_element_type=jnp.float32,
            )
            sums[p] = term if sums[p] is None else sums[p] + term
    for p in range(group // 2):
        if not last:
            after[p] = sums[p]
            continue
        for out, at in ((even, 0), (odd, 1)):
            out[p] = jnp.concatenate(
                [
                    sums[p][
                        (at * local_blocks + j) * BLOCK : (at * local_blocks + j + 1) * BLOCK,
                        (at * local_blocks + j) * rank : (at * local_blocks + j + 1) * rank,
                    ]
                    for j in range(local_blocks)
                ],
                1,
            )


def final_kernel(rows, rank, bases, lows, *refs):
    lists, refs = refs[:3], refs[3:]
    base_refs, refs = refs[:bases], refs[bases:]
    low_refs, refs = refs[:lows], refs[lows:]
    ups, out, up_here, sems = refs
    local_blocks = rows // BLOCK
    me = lax.axis_index("batch")
    found = [table(lists, me * local_blocks + j) for j in range(local_blocks)]
    copies = run_copies([(ups.at[found[j][1]], up_here.at[j]) for j in range(local_blocks)], sems)
    low = low_refs[0][...]
    for ref in low_refs[1:]:
        low = low + ref[...]
    low = low.astype(jnp.bfloat16)
    for j in range(local_blocks):
        copies[j].wait()
        here = pl.ds(j * BLOCK, BLOCK)
        total = jnp.dot(
            low[:, j * rank : (j + 1) * rank], up_here[j], preferred_element_type=jnp.float32
        )
        for ref in base_refs:
            total = total + ref[here, :].astype(jnp.float32)
        live = lax.broadcasted_iota(jnp.int32, total.shape, 0) < found[j][2]
        out[here, :] = jnp.where(live, total, 0.0).astype(jnp.bfloat16)


def layer_sums(values, narrow):
    parts = [[v] for v in values]
    bit = 1
    while len(parts) > 1:
        kept = []
        for mine, theirs in zip(parts[0::2], parts[1::2]):
            sent = functools.reduce(lambda a, b: a + b.astype(a.dtype), theirs)
            if narrow and bit > 1:
                sent = sent.astype(jnp.bfloat16)
            kept.append(mine + [swap(sent, "batch", bit)])
        parts = kept
        bit *= 2
    return parts[0]


def shards(
    tokens,
    key_matrix,
    adapter_down_factors,
    adapter_up_factors,
    request_block_list,
    request_adapter_index,
    request_tail_tokens,
):
    rows, width = tokens.shape
    depth, out_width = key_matrix.shape
    adapters, rank = adapter_down_factors.shape[1:]
    reps, devices = lax.axis_size("rep"), lax.axis_size("batch")
    group = 2 * LAYER_CHIPS // reps
    layers = devices // group
    splits = reps if (depth // reps) % LANES == 0 else 1
    part = depth // splits
    local_blocks = rows // BLOCK
    held_width = layers * depth
    lists = (request_block_list, request_adapter_index, request_tail_tokens)
    f32, bf16 = jnp.float32, jnp.bfloat16

    if splits > 1:
        key_parts = call(
            functools.partial(key_parts_kernel, splits, part),
            [jax.ShapeDtypeStruct((part, out_width), bf16)] * splits,
            [HBM] * splits,
            [HBM],
            [pltpu.SemaphoreType.DMA((splits,))],
            0,
            4 * depth * out_width,
        )(key_matrix)
    else:
        key_parts = [key_matrix]

    def over_layers(own):
        bundles = []
        bit = layers // 2
        while bit:
            moved = [([bit], swap(own, "batch", bit * group))]
            if bundles:
                rest = [v for _, v in bundles]
                rest = rest[0] if len(rest) == 1 else jnp.concatenate(rest, 0)
                order = [t ^ bit for ts, _ in bundles for t in ts]
                moved.append((order, swap(rest, "batch", bit * group)))
            bundles = bundles + moved
            bit //= 2
        return bundles

    key_bundles = over_layers(key_parts[0])

    pieces = call(
        functools.partial(token_pieces_kernel, group, layers, splits, part),
        [jax.ShapeDtypeStruct((rows, held_width), bf16)] * group,
        [HBM] * group,
        [HBM],
        [pltpu.SemaphoreType.DMA((group * layers * splits,))],
        0,
        4 * rows * width,
    )(tokens)
    pieces = [pieces[0]] + [swap(pieces[s], "batch", s) for s in range(1, group)]

    down = jnp.transpose(adapter_down_factors, (1, 2, 0))
    requests = request_adapter_index.shape[0]
    by_request = requests < adapters
    slots = requests if by_request else adapters
    if by_request:
        down = call(
            functools.partial(chosen_kernel, slots, rank, splits, part),
            jax.ShapeDtypeStruct((slots * rank, depth), bf16),
            HBM,
            [SMEM, HBM],
            [pltpu.SemaphoreType.DMA((slots * splits,))],
            0,
            4 * slots * rank * depth,
        )(request_adapter_index, down)
    else:
        down = down.reshape(slots * rank, depth)
    down, _ = lax.optimization_barrier((down, key_bundles[0][1]))
    down_bundles = over_layers(down)

    arrays, entries = [], []
    for ts, value in [([0], None)] + key_bundles:
        for h in range(splits):
            if value is None:
                arrays.append(key_parts[h])
            else:
                arrays.append(swap(value, "rep", h) if h else value)
            for i, t in enumerate(ts):
                entries.append((t, len(arrays) - 1, i * part, part, t * depth + h * part))
    partial_sums = [None] * group
    for p in range(group // 2):
        partial_sums[2 * p : 2 * p + 2] = call(
            functools.partial(base_kernel, rows, depth, layers, tuple(entries), len(arrays)),
            [jax.ShapeDtypeStruct((rows, out_width), f32)] * 2,
            [VMEM] * 2,
            [HBM] * (2 + len(arrays)),
            [pltpu.VMEM((2 * rows, held_width), bf16)]
            + [pltpu.VMEM(a.shape, bf16) for a in arrays]
            + [pltpu.SemaphoreType.DMA((2, layers)), pltpu.SemaphoreType.DMA((len(arrays),))],
            4 * rows * held_width * out_width,
            2 * held_width * (2 * rows + out_width) + 8 * rows * out_width,
        )(pieces[2 * p], pieces[2 * p + 1], *arrays)
    bases = layer_sums(partial_sums, True)

    def low_call(bundles, before, last):
        taken = [value for _, value in bundles]
        at = [
            (t, a, i * slots * rank) for a, (ts, _) in enumerate(bundles) for i, t in enumerate(ts)
        ]
        pairs, tall, wide = group // 2, 2 * rows, 2 * local_blocks * rank
        if last:
            outs = [jax.ShapeDtypeStruct((pairs, BLOCK, local_blocks * rank), f32)] * 2
            out_specs = [VMEM] * 2
        else:
            outs, out_specs = jax.ShapeDtypeStruct((pairs, tall, wide), f32), VMEM
        return call(
            functools.partial(
                low_kernel, group, rows, depth, rank, tuple(at), len(taken), by_request,
                before is not None, last,
            ),
            outs,
            out_specs,
            [SMEM] * 3 + [HBM] * (group + len(taken)) + [VMEM] * (before is not None),
            [pltpu.VMEM((group * rows, len(at) * depth), bf16)]
            + [pltpu.VMEM(v.shape, bf16) for v in taken]
            + [pltpu.SemaphoreType.DMA((group, len(at))), pltpu.SemaphoreType.DMA((len(taken),))],
            2 * pairs * tall * wide * len(at) * depth,
            2 * len(at) * depth * (group * rows + slots * rank) + 4 * pairs * tall * wide,
        )(*lists, *pieces, *taken, *([before] if before is not None else []))

    early = low_call([([0], down)] + down_bundles[:-1], None, False)
    even, odd = low_call(down_bundles[-1:], early, True)
    got = swap(odd, "batch", 1)
    lows = layer_pairs(even, got)

    return call(
        functools.partial(final_kernel, rows, rank, len(bases), len(lows)),
        jax.ShapeDtypeStruct((rows, out_width), bf16),
        VMEM,
        [SMEM] * 3 + [VMEM] * (len(bases) + len(lows)) + [HBM],
        [pltpu.VMEM((local_blocks, rank, out_width), bf16), pltpu.SemaphoreType.DMA((local_blocks,))],
        2 * rows * rank * out_width,
        8 * rows * out_width,
    )(*lists, *bases, *lows, adapter_up_factors)


def layer_pairs(mine, got):
    bit = 2
    while mine.shape[0] > 1:
        total = mine + got
        mine, got = total[0::2], swap(total[1::2], "batch", bit)
        bit *= 2
    return [mine[0], got[0]]


def solution(mesh):
    placed = (
        P(("rep", "batch"), None),
        P("batch", None),
        P("batch", None, None),
        P(),
        P("rep"),
        P("rep"),
        P("rep"),
    )
    return jax.shard_map(
        shards, mesh=mesh, in_specs=placed, out_specs=P(("rep", "batch"), None), check_vma=False
    )
```

```python
import functools

import jax
import jax.numpy as jnp
from jax import lax
from jax.experimental import pallas as pl
from jax.experimental.pallas import tpu as pltpu
from jax.sharding import PartitionSpec as P

BLOCK = 128
LANES = 128
MOST = 16
LAYER_CHIPS = 4
VMEM_BYTES = 28 * 1024 * 1024
FIRST_VMEM_BYTES = 56 * 1024 * 1024

HBM = pl.BlockSpec(memory_space=pl.ANY)
VMEM = pl.BlockSpec(memory_space=pltpu.VMEM)
SMEM = pl.BlockSpec(memory_space=pltpu.SMEM)


def call(kernel, outs, out_specs, in_specs, scratch, flops, moved, vmem=VMEM_BYTES):
    return pl.pallas_call(
        kernel,
        out_shape=outs,
        in_specs=in_specs,
        out_specs=out_specs,
        scratch_shapes=scratch,
        compiler_params=pltpu.CompilerParams(vmem_limit_bytes=vmem),
        cost_estimate=pl.CostEstimate(flops=flops, bytes_accessed=moved, transcendentals=0),
    )


def swap(value, axis, bit):
    return lax.ppermute(value, axis, [(i, i ^ bit) for i in range(lax.axis_size(axis))])


def run_copies(pairs, sems):
    copies = [pltpu.make_async_copy(a, b, sems.at[i]) for i, (a, b) in enumerate(pairs)]
    for copy in copies:
        copy.start()
    return copies


def part_start(h, part):
    return pl.multiple_of((lax.axis_index("rep") ^ h) * part, part)


def first_kernel(group, layers, splits, part, key, tokens, *refs):
    keys, refs = refs[:splits], refs[splits:]
    outs, sems = refs[:group], refs[group]
    depth = splits * part
    me = lax.axis_index("batch")
    layer, spot = me // group, me % group
    pairs = [(key.at[pl.ds(part_start(h, part), part), :], keys[h]) for h in range(splits)]
    for s in reversed(range(group)):
        for t in range(layers):
            first = ((layer ^ t) * group + (spot ^ s)) * depth
            for h in range(splits):
                start = first + part_start(h, part) if splits > 1 else first
                start = pl.multiple_of(start, part)
                pairs.append(
                    (
                        tokens.at[:, pl.ds(start, part)],
                        outs[s].at[:, pl.ds(t * depth + h * part, part)],
                    )
                )
    for copy in run_copies(pairs, sems):
        copy.wait()


def gate_kernel(value, *refs):
    pass


def gate(value, *ready):
    return pl.pallas_call(
        gate_kernel,
        out_shape=jax.ShapeDtypeStruct(value.shape, value.dtype),
        in_specs=[HBM] * (1 + len(ready)),
        out_specs=HBM,
        input_output_aliases={0: 0},
    )(value, *ready)


def chosen_kernel(slots, rank, splits, part, group, layers, shift, picks, down, *refs):
    outs, sems = refs[:-1], refs[-1]
    layer = lax.axis_index("batch") // group
    half = (layer * 2) // layers
    pairs = []
    for n, out in enumerate(outs):
        first = (half ^ 1 ^ n) * shift
        for q in range(slots):
            for h in range(splits):
                start = part_start(h, part) if splits > 1 else 0
                pairs.append(
                    (
                        down.at[picks[first + q], :, pl.ds(start, part)],
                        out.at[pl.ds(q * rank, rank), pl.ds(h * part, part)],
                    )
                )
    for copy in run_copies(pairs, sems):
        copy.wait()


def base_kernel(rows, tokens_of, moves, count, *refs):
    toks, arrays = refs[:tokens_of], refs[tokens_of : tokens_of + count]
    outs = refs[tokens_of + count : 2 * tokens_of + count]
    held, weights, sems = refs[2 * tokens_of + count :]
    pairs = [(tok, held.at[pl.ds(i * rows, rows), :]) for i, tok in enumerate(toks)]
    for a, row, deep, to in moves:
        pairs.append((arrays[a].at[pl.ds(row, deep), :], weights.at[pl.ds(to, deep), :]))
    for copy in run_copies(pairs, sems):
        copy.wait()
    width = weights.shape[1]
    step = 2 * LANES if width % (2 * LANES) == 0 else width
    for column in range(0, width, step):
        here = pl.ds(column, step)
        total = jnp.dot(held[...], weights[:, here], preferred_element_type=jnp.float32)
        for i in range(tokens_of):
            outs[i][:, here] = total[i * rows : (i + 1) * rows]


def table(lists, block):
    sizes, adapters, tails = lists
    end = jnp.int32(0)
    owner, adapter, limit = jnp.int32(0), jnp.int32(0), jnp.int32(BLOCK)
    for q in range(sizes.shape[0]):
        begin = end
        end = end + sizes[q]
        inside = (begin <= block) & (block < end)
        owner = jnp.where(inside, q, owner)
        adapter = jnp.where(inside, adapters[q], adapter)
        limit = jnp.where(inside & (block == end - 1), tails[q], limit)
    return owner, adapter, limit


def low_kernel(
    group, layers, rows, depth, rank, entries, count, by_request, shift, has_sum, last, *refs
):
    lists, refs = refs[:3], refs[3:]
    toks, refs = refs[:group], refs[group:]
    arrays, refs = refs[:count], refs[count:]
    if has_sum:
        before, refs = refs[0], refs[1:]
    if last:
        even, odd, refs = refs[0], refs[1], refs[2:]
    else:
        after, refs = refs[0], refs[1:]
    held, refs = refs[0], refs[1:]
    downs, refs = refs[:count], refs[count:]
    tok_sems, sems = refs
    local_blocks = rows // BLOCK
    me = lax.axis_index("batch")
    layer, spot = me // group, me % group
    first = {}
    started = {}
    for n, (t, a, _) in enumerate(entries):
        if a not in started:
            started[a] = pltpu.make_async_copy(arrays[a], downs[a], sems.at[a])
            started[a].start()
        first[t] = []
        for s in range(group):
            copy = pltpu.make_async_copy(
                toks[s].at[:, pl.ds(t * depth, depth)],
                held.at[pl.ds(s * rows, rows), pl.ds(n * depth, depth)],
                tok_sems.at[s, n],
            )
            copy.start()
            first[t].append(copy)
    slots = []
    for s in range(group):
        for j in range(local_blocks):
            block = (layer * group + (spot ^ s)) * local_blocks + j
            owner, adapter, _ = table(lists, block)
            slots.append(owner - (layer * 2) // layers * shift if by_request else adapter)
    ready = set()
    wide = 2 * local_blocks
    sums = [before[p] if has_sum else None for p in range(group // 2)]
    for n, (t, a, row) in enumerate(entries):
        for copy in first[t]:
            copy.wait()
        if a not in ready:
            started[a].wait()
            ready.add(a)
        for p in range(group // 2):
            chosen = jnp.concatenate(
                [
                    downs[a][pl.ds(pl.multiple_of(row + slots[p * wide + i] * rank, rank), rank), :]
                    for i in range(wide)
                ],
                0,
            )
            term = lax.dot_general(
                held[2 * p * rows : 2 * (p + 1) * rows, n * depth : (n + 1) * depth],
                chosen,
                (((1,), (1,)), ((), ())),
                preferred_element_type=jnp.float32,
            )
            sums[p] = term if sums[p] is None else sums[p] + term
    for p in range(group // 2):
        if not last:
            after[p] = sums[p]
            continue
        for out, at in ((even, 0), (odd, 1)):
            out[p] = jnp.concatenate(
                [
                    sums[p][
                        (at * local_blocks + j) * BLOCK : (at * local_blocks + j + 1) * BLOCK,
                        (at * local_blocks + j) * rank : (at * local_blocks + j + 1) * rank,
                    ]
                    for j in range(local_blocks)
                ],
                1,
            )


def final_kernel(rows, rank, bases, lows, *refs):
    lists, refs = refs[:3], refs[3:]
    base_refs, refs = refs[:bases], refs[bases:]
    low_refs, refs = refs[:lows], refs[lows:]
    ups, out, up_here, sems = refs
    local_blocks = rows // BLOCK
    me = lax.axis_index("batch")
    found = [table(lists, me * local_blocks + j) for j in range(local_blocks)]
    copies = run_copies([(ups.at[found[j][1]], up_here.at[j]) for j in range(local_blocks)], sems)
    low = low_refs[0][...]
    for ref in low_refs[1:]:
        low = low + ref[...]
    low = low.astype(jnp.bfloat16)
    for j in range(local_blocks):
        copies[j].wait()
        here = pl.ds(j * BLOCK, BLOCK)
        total = jnp.dot(
            low[:, j * rank : (j + 1) * rank], up_here[j], preferred_element_type=jnp.float32
        )
        for ref in base_refs:
            total = total + ref[here, :].astype(jnp.float32)
        live = lax.broadcasted_iota(jnp.int32, total.shape, 0) < found[j][2]
        out[here, :] = jnp.where(live, total, 0.0).astype(jnp.bfloat16)


def layer_sums(values, narrow):
    parts = [[v] for v in values]
    bit = 1
    while len(parts) > 1:
        kept = []
        for mine, theirs in zip(parts[0::2], parts[1::2]):
            sent = functools.reduce(lambda a, b: a + b.astype(a.dtype), theirs)
            if narrow and bit > 1:
                sent = sent.astype(jnp.bfloat16)
            kept.append(mine + [swap(sent, "batch", bit)])
        parts = kept
        bit *= 2
    return parts[0]


def shards(
    tokens,
    key_matrix,
    adapter_down_factors,
    adapter_up_factors,
    request_block_list,
    request_adapter_index,
    request_tail_tokens,
):
    rows, width = tokens.shape
    depth, out_width = key_matrix.shape
    adapters, rank = adapter_down_factors.shape[1:]
    reps, devices = lax.axis_size("rep"), lax.axis_size("batch")
    group = 2 * LAYER_CHIPS // reps
    layers = devices // group
    splits = reps if (depth // reps) % LANES == 0 else 1
    part = depth // splits
    local_blocks = rows // BLOCK
    held_width = layers * depth
    lists = (request_block_list, request_adapter_index, request_tail_tokens)
    f32, bf16 = jnp.float32, jnp.bfloat16

    first = call(
        functools.partial(first_kernel, group, layers, splits, part),
        [jax.ShapeDtypeStruct((part, out_width), bf16)] * splits
        + [jax.ShapeDtypeStruct((rows, held_width), bf16)] * group,
        [HBM] * (splits + group),
        [HBM] * 2,
        [pltpu.SemaphoreType.DMA((splits + group * layers * splits,))],
        0,
        4 * (rows * width + depth * out_width),
        FIRST_VMEM_BYTES,
    )(key_matrix, tokens)
    key_parts, pieces = first[:splits], list(first[splits:])

    def over_layers(across, near):
        bundles = []
        bit = layers // 2
        while bit:
            own = near(bundles) if bundles else across
            moved = [([bit], swap(own, "batch", bit * group))]
            if bundles:
                rest = [v for _, v in bundles]
                rest = rest[0] if len(rest) == 1 else jnp.concatenate(rest, 0)
                order = [t ^ bit for ts, _ in bundles for t in ts]
                moved.append((order, swap(rest, "batch", bit * group)))
            bundles = bundles + moved
            bit //= 2
        return bundles

    key_bundles = over_layers(key_parts[0], lambda _: key_parts[0])

    for s in reversed(range(1, group)):
        if 1 < s < group - 1:
            pieces[s] = gate(pieces[s], pieces[s + 1])
        pieces[s] = swap(pieces[s], "batch", s)

    down = jnp.transpose(adapter_down_factors, (1, 2, 0))
    requests = request_adapter_index.shape[0]
    by_request = requests < adapters
    shift = 1 if by_request and local_blocks * devices == 2 * MOST and layers > 1 else 0
    slots = requests - shift if by_request else adapters
    if by_request:
        across, down = call(
            functools.partial(chosen_kernel, slots, rank, splits, part, group, layers, shift),
            [jax.ShapeDtypeStruct((slots * rank, depth), bf16)] * 2,
            [HBM] * 2,
            [SMEM, HBM],
            [pltpu.SemaphoreType.DMA((2 * slots * splits,))],
            0,
            8 * slots * rank * depth,
            FIRST_VMEM_BYTES,
        )(request_adapter_index, down)
    else:
        down = down.reshape(slots * rank, depth)
        across = down
    across = gate(across, key_bundles[0][1])
    down = gate(down, key_bundles[-1][1])
    down_bundles = over_layers(across, lambda _: down)

    arrays, moves = [], []
    for ts, value in [([0], None)] + key_bundles:
        if value is None:
            arrays.extend(key_parts)
        else:
            arrays.append(value)
        for i, t in enumerate(ts):
            moves.append((len(arrays) - (splits if value is None else 1), i * part, part, t * depth))
    for h in range(1, splits):
        moves.append((h, 0, part, h * part))
        for taken in (key_bundles[:1], key_bundles[1:]):
            if taken:
                values = [v for _, v in taken]
                values = values[0] if len(values) == 1 else jnp.concatenate(values, 0)
                arrays.append(swap(values, "rep", h))
                for i, t in enumerate([t for ts, _ in taken for t in ts]):
                    moves.append((len(arrays) - 1, i * part, part, t * depth + h * part))
    partial_sums = [None] * group
    late = [2] if group > 2 else []
    for which in ([s for s in range(group) if s not in late], late):
        if not which:
            continue
        results = call(
            functools.partial(base_kernel, rows, len(which), tuple(moves), len(arrays)),
            [jax.ShapeDtypeStruct((rows, out_width), f32)] * len(which),
            [VMEM] * len(which),
            [HBM] * (len(which) + len(arrays)),
            [
                pltpu.VMEM((len(which) * rows, held_width), bf16),
                pltpu.VMEM((held_width, out_width), bf16),
                pltpu.SemaphoreType.DMA((len(which) + len(moves),)),
            ],
            2 * len(which) * rows * held_width * out_width,
            2 * held_width * (len(which) * rows + out_width) + 4 * len(which) * rows * out_width,
        )(*[pieces[s] for s in which], *arrays)
        for s, value in zip(which, results):
            partial_sums[s] = value
    bases = layer_sums(partial_sums, True)

    def low_call(bundles, before, last):
        taken = [value for _, value in bundles]
        at = [
            (t, a, i * slots * rank) for a, (ts, _) in enumerate(bundles) for i, t in enumerate(ts)
        ]
        pairs, tall, wide = group // 2, 2 * rows, 2 * local_blocks * rank
        if last:
            outs = [jax.ShapeDtypeStruct((pairs, BLOCK, local_blocks * rank), f32)] * 2
            out_specs = [VMEM] * 2
        else:
            outs, out_specs = jax.ShapeDtypeStruct((pairs, tall, wide), f32), VMEM
        return call(
            functools.partial(
                low_kernel, group, layers, rows, depth, rank, tuple(at), len(taken), by_request,
                shift, before is not None, last,
            ),
            outs,
            out_specs,
            [SMEM] * 3 + [HBM] * (group + len(taken)) + [VMEM] * (before is not None),
            [pltpu.VMEM((group * rows, len(at) * depth), bf16)]
            + [pltpu.VMEM(v.shape, bf16) for v in taken]
            + [pltpu.SemaphoreType.DMA((group, len(at))), pltpu.SemaphoreType.DMA((len(taken),))],
            2 * pairs * tall * wide * len(at) * depth,
            2 * len(at) * depth * (group * rows + slots * rank) + 4 * pairs * tall * wide,
        )(*lists, *pieces, *taken, *([before] if before is not None else []))

    early = low_call([([0], down)] + down_bundles[:-1], None, False)
    even, odd = low_call(down_bundles[-1:], early, True)
    got = swap(odd, "batch", 1)
    lows = layer_pairs(even, got)

    return call(
        functools.partial(final_kernel, rows, rank, len(bases), len(lows)),
        jax.ShapeDtypeStruct((rows, out_width), bf16),
        VMEM,
        [SMEM] * 3 + [VMEM] * (len(bases) + len(lows)) + [HBM],
        [pltpu.VMEM((local_blocks, rank, out_width), bf16), pltpu.SemaphoreType.DMA((local_blocks,))],
        2 * rows * rank * out_width,
        8 * rows * out_width,
    )(*lists, *bases, *lows, adapter_up_factors)


def layer_pairs(mine, got):
    bit = 2
    while mine.shape[0] > 1:
        total = mine + got
        mine, got = total[0::2], swap(total[1::2], "batch", bit)
        bit *= 2
    return [mine[0], got[0]]


def solution(mesh):
    placed = (
        P(("rep", "batch"), None),
        P("batch", None),
        P("batch", None, None),
        P(),
        P("rep"),
        P("rep"),
        P("rep"),
    )
    return jax.shard_map(
        shards, mesh=mesh, in_specs=placed, out_specs=P(("rep", "batch"), None), check_vma=False
    )
```

```python
import functools

import jax
import jax.numpy as jnp
from jax import lax
from jax.experimental import pallas as pl
from jax.experimental.pallas import tpu as pltpu
from jax.sharding import PartitionSpec as P

BLOCK = 128
LANES = 128
MOST = 16
LAYER_CHIPS = 4
VMEM_BYTES = 28 * 1024 * 1024
CORE_FLOPS_PER_US = 1_153_500_000

HBM = pl.BlockSpec(memory_space=pl.ANY)
VMEM = pl.BlockSpec(memory_space=pltpu.VMEM)
SMEM = pl.BlockSpec(memory_space=pltpu.SMEM)


def call(kernel, outs, out_specs, in_specs, scratch, flops, moved):
    return pl.pallas_call(
        kernel,
        out_shape=outs,
        in_specs=in_specs,
        out_specs=out_specs,
        scratch_shapes=scratch,
        compiler_params=pltpu.CompilerParams(vmem_limit_bytes=VMEM_BYTES),
        cost_estimate=pl.CostEstimate(flops=flops, bytes_accessed=moved, transcendentals=0),
    )


def swap(value, axis, bit):
    return lax.ppermute(value, axis, [(i, i ^ bit) for i in range(lax.axis_size(axis))])


def run_copies(pairs, sems):
    copies = [pltpu.make_async_copy(a, b, sems.at[i]) for i, (a, b) in enumerate(pairs)]
    for copy in copies:
        copy.start()
    return copies


def part_start(h, part):
    return pl.multiple_of((lax.axis_index("rep") ^ h) * part, part)


def first_kernel(group, layers, splits, part, key, tokens, *refs):
    keys, refs = refs[:splits], refs[splits:]
    outs, sems = refs[:-1], refs[-1]
    rows = tokens.shape[0]
    depth = splits * part
    me = lax.axis_index("batch")
    layer, spot = me // group, me % group
    pairs = [(key.at[pl.ds(part_start(h, part), part), :], keys[h]) for h in range(splits)]
    for s in reversed(range(group)):
        for t in range(layers):
            first = ((layer ^ t) * group + (spot ^ s)) * depth
            for h in range(splits):
                start = first + part_start(h, part) if splits > 1 else first
                start = pl.multiple_of(start, part)
                to = pl.ds(t * depth + h * part, part)
                if s < 2:
                    there = outs[s].at[:, to]
                else:
                    there = outs[2].at[pl.ds((s - 2) * rows, rows), to]
                pairs.append((tokens.at[:, pl.ds(start, part)], there))
    for copy in run_copies(pairs, sems):
        copy.wait()


def gate_kernel(value, *refs):
    pass


def gate(value, *ready, us=0):
    return pl.pallas_call(
        gate_kernel,
        out_shape=jax.ShapeDtypeStruct(value.shape, value.dtype),
        in_specs=[HBM] * (1 + len(ready)),
        out_specs=HBM,
        input_output_aliases={0: 0},
        cost_estimate=pl.CostEstimate(
            flops=us * CORE_FLOPS_PER_US, bytes_accessed=0, transcendentals=0
        ),
    )(value, *ready)


def chosen_kernel(slots, rank, splits, part, group, layers, shift, picks, down, *refs):
    outs, sems = refs[:-1], refs[-1]
    layer = lax.axis_index("batch") // group
    half = (layer * 2) // layers
    pairs = []
    for n, out in enumerate(outs):
        first = (half ^ 1 ^ n) * shift
        for q in range(slots):
            for h in range(splits):
                start = part_start(h, part) if splits > 1 else 0
                pairs.append(
                    (
                        down.at[picks[first + q], :, pl.ds(start, part)],
                        out.at[pl.ds(q * rank, rank), pl.ds(h * part, part)],
                    )
                )
    for copy in run_copies(pairs, sems):
        copy.wait()


def base_kernel(rows, tokens_of, moves, count, *refs):
    toks, arrays = refs[:tokens_of], refs[tokens_of : tokens_of + count]
    outs = refs[tokens_of + count : 2 * tokens_of + count]
    held, weights, sems = refs[2 * tokens_of + count :]
    deep, width = weights.shape
    halves = [(0, deep // 2), (deep // 2, deep)]
    waits = []
    for begin, end in halves:
        pairs = [
            (tok.at[:, pl.ds(begin, end - begin)], held.at[pl.ds(i * rows, rows), pl.ds(begin, end - begin)])
            for i, tok in enumerate(toks)
        ]
        for a, row, rows_of, to in moves:
            if begin <= to < end:
                pairs.append((arrays[a].at[pl.ds(row, rows_of), :], weights.at[pl.ds(to, rows_of), :]))
        first = sum(len(w) for w in waits)
        waits.append(run_copies(pairs, sems.at[pl.ds(first, len(pairs))]))
    step = 2 * LANES if width % (2 * LANES) == 0 else width
    for copies, (begin, end) in zip(waits, halves):
        for copy in copies:
            copy.wait()
        for column in range(0, width, step):
            here = pl.ds(column, step)
            total = jnp.dot(
                held[:, begin:end], weights[begin:end, here], preferred_element_type=jnp.float32
            )
            for i in range(tokens_of):
                mine = total[i * rows : (i + 1) * rows]
                if begin == 0:
                    outs[i][:, here] = mine
                else:
                    outs[i][:, here] += mine


def table(lists, block):
    sizes, adapters, tails = lists
    end = jnp.int32(0)
    owner, adapter, limit = jnp.int32(0), jnp.int32(0), jnp.int32(BLOCK)
    for q in range(sizes.shape[0]):
        begin = end
        end = end + sizes[q]
        inside = (begin <= block) & (block < end)
        owner = jnp.where(inside, q, owner)
        adapter = jnp.where(inside, adapters[q], adapter)
        limit = jnp.where(inside & (block == end - 1), tails[q], limit)
    return owner, adapter, limit


def low_kernel(
    group, layers, rows, depth, rank, entries, count, by_request, shift, has_sum, last, *refs
):
    lists, refs = refs[:3], refs[3:]
    toks, refs = refs[:group], refs[group:]
    arrays, refs = refs[:count], refs[count:]
    if has_sum:
        before, refs = refs[0], refs[1:]
    if last:
        even, odd, refs = refs[0], refs[1], refs[2:]
    else:
        after, refs = refs[0], refs[1:]
    held, refs = refs[0], refs[1:]
    downs, refs = refs[:count], refs[count:]
    tok_sems, sems = refs
    local_blocks = rows // BLOCK
    me = lax.axis_index("batch")
    layer, spot = me // group, me % group
    first = {}
    started = {}
    for n, (t, a, _) in enumerate(entries):
        if a not in started:
            started[a] = pltpu.make_async_copy(arrays[a], downs[a], sems.at[a])
            started[a].start()
        first[t] = []
        for s in range(group):
            copy = pltpu.make_async_copy(
                toks[s].at[:, pl.ds(t * depth, depth)],
                held.at[pl.ds(s * rows, rows), pl.ds(n * depth, depth)],
                tok_sems.at[s, n],
            )
            copy.start()
            first[t].append(copy)
    slots = []
    for s in range(group):
        for j in range(local_blocks):
            block = (layer * group + (spot ^ s)) * local_blocks + j
            owner, adapter, _ = table(lists, block)
            slots.append(owner - (layer * 2) // layers * shift if by_request else adapter)
    ready = set()
    wide = 2 * local_blocks
    sums = [before[p] if has_sum else None for p in range(group // 2)]
    for n, (t, a, row) in enumerate(entries):
        for copy in first[t]:
            copy.wait()
        if a not in ready:
            started[a].wait()
            ready.add(a)
        for p in range(group // 2):
            chosen = jnp.concatenate(
                [
                    downs[a][pl.ds(pl.multiple_of(row + slots[p * wide + i] * rank, rank), rank), :]
                    for i in range(wide)
                ],
                0,
            )
            term = lax.dot_general(
                held[2 * p * rows : 2 * (p + 1) * rows, n * depth : (n + 1) * depth],
                chosen,
                (((1,), (1,)), ((), ())),
                preferred_element_type=jnp.float32,
            )
            sums[p] = term if sums[p] is None else sums[p] + term
    for p in range(group // 2):
        if not last:
            after[p] = sums[p]
            continue
        for out, at in ((even, 0), (odd, 1)):
            out[p] = jnp.concatenate(
                [
                    sums[p][
                        (at * local_blocks + j) * BLOCK : (at * local_blocks + j + 1) * BLOCK,
                        (at * local_blocks + j) * rank : (at * local_blocks + j + 1) * rank,
                    ]
                    for j in range(local_blocks)
                ],
                1,
            )


def final_kernel(rows, rank, bases, lows, *refs):
    lists, refs = refs[:3], refs[3:]
    base_refs, refs = refs[:bases], refs[bases:]
    low_refs, refs = refs[:lows], refs[lows:]
    ups, out, up_here, sems = refs
    local_blocks = rows // BLOCK
    me = lax.axis_index("batch")
    found = [table(lists, me * local_blocks + j) for j in range(local_blocks)]
    copies = run_copies([(ups.at[found[j][1]], up_here.at[j]) for j in range(local_blocks)], sems)
    low = low_refs[0][...]
    for ref in low_refs[1:]:
        low = low + ref[...]
    low = low.astype(jnp.bfloat16)
    for j in range(local_blocks):
        copies[j].wait()
        here = pl.ds(j * BLOCK, BLOCK)
        total = jnp.dot(
            low[:, j * rank : (j + 1) * rank], up_here[j], preferred_element_type=jnp.float32
        )
        for ref in base_refs:
            total = total + ref[here, :].astype(jnp.float32)
        live = lax.broadcasted_iota(jnp.int32, total.shape, 0) < found[j][2]
        out[here, :] = jnp.where(live, total, 0.0).astype(jnp.bfloat16)


def layer_sums(values, narrow):
    parts = [[v] for v in values]
    bit = 1
    while len(parts) > 1:
        kept = []
        for mine, theirs in zip(parts[0::2], parts[1::2]):
            sent = functools.reduce(lambda a, b: a + b.astype(a.dtype), theirs)
            if narrow and bit > 1:
                sent = sent.astype(jnp.bfloat16)
            kept.append(mine + [swap(sent, "batch", bit)])
        parts = kept
        bit *= 2
    return parts[0]


def shards(
    tokens,
    key_matrix,
    adapter_down_factors,
    adapter_up_factors,
    request_block_list,
    request_adapter_index,
    request_tail_tokens,
):
    rows, width = tokens.shape
    depth, out_width = key_matrix.shape
    adapters, rank = adapter_down_factors.shape[1:]
    reps, devices = lax.axis_size("rep"), lax.axis_size("batch")
    group = 2 * LAYER_CHIPS // reps
    layers = devices // group
    splits = reps if (depth // reps) % LANES == 0 else 1
    part = depth // splits
    local_blocks = rows // BLOCK
    held_width = layers * depth
    lists = (request_block_list, request_adapter_index, request_tail_tokens)
    f32, bf16 = jnp.float32, jnp.bfloat16

    first = call(
        functools.partial(first_kernel, group, layers, splits, part),
        [jax.ShapeDtypeStruct((part, out_width), bf16)] * splits
        + [jax.ShapeDtypeStruct((rows, held_width), bf16)] * 2
        + [jax.ShapeDtypeStruct(((group - 2) * rows, held_width), bf16)] * (group > 2),
        [HBM] * (splits + 2 + (group > 2)),
        [HBM] * 2,
        [pltpu.SemaphoreType.DMA((splits + group * layers * splits,))],
        0,
        4 * (rows * width + depth * out_width),
    )(key_matrix, tokens)
    key_parts = first[:splits]
    if group > 2:
        far = swap(first[splits + 2], "batch", 2)
    pieces = [first[splits], swap(first[splits + 1], "batch", 1)]

    def over_layers(across, near, after):
        bundles = []
        bit = layers // 2
        while bit:
            own = near(bundles) if bundles else across
            moved = [([bit], swap(own, "batch", bit * group))]
            if bundles:
                rest = [v for _, v in bundles]
                rest = rest[0] if len(rest) == 1 else jnp.concatenate(rest, 0)
                order = [t ^ bit for ts, _ in bundles for t in ts]
                moved.append((order, swap(rest, "batch", bit * group)))
            else:
                moved = [([bit], after(moved[0][1]))]
            bundles = bundles + moved
            bit //= 2
        return bundles

    key_bundles = over_layers(
        key_parts[0], lambda _: key_parts[0], lambda v: gate(v, pieces[1], us=2)
    )
    key_swaps, last_keys = [], key_bundles[-1][1]
    for h in range(1, splits):
        for taken in (key_bundles[:1], key_bundles[1:]):
            if taken:
                values = [v for _, v in taken]
                values = values[0] if len(values) == 1 else jnp.concatenate(values, 0)
                if key_swaps:
                    values = gate(values, key_swaps[-1][2], us=2)
                    last_keys = values
                key_swaps.append((h, [t for ts, _ in taken for t in ts], swap(values, "rep", h)))

    down = jnp.transpose(adapter_down_factors, (1, 2, 0))
    requests = request_adapter_index.shape[0]
    by_request = requests < adapters
    shift = 1 if by_request and local_blocks * devices == 2 * MOST and layers > 1 else 0
    slots = requests - shift if by_request else adapters
    if by_request:
        across, down = call(
            functools.partial(chosen_kernel, slots, rank, splits, part, group, layers, shift),
            [jax.ShapeDtypeStruct((slots * rank, depth), bf16)] * 2,
            [HBM] * 2,
            [SMEM, HBM],
            [pltpu.SemaphoreType.DMA((2 * slots * splits,))],
            0,
            8 * slots * rank * depth,
        )(request_adapter_index, down)
    else:
        down = down.reshape(slots * rank, depth)
        across = down
    across = gate(across, key_bundles[0][1])
    down = gate(down, last_keys)
    down_bundles = over_layers(across, lambda _: down, lambda v: gate(v, us=10))
    if group > 2:
        far = gate(far, *[v for _, v in down_bundles[:2]], *[v for _, _, v in key_swaps], us=2)
        pieces += [far[:rows], swap(far[rows:], "batch", 1)]

    arrays, moves = [], []
    for ts, value in [([0], None)] + key_bundles:
        if value is None:
            arrays.extend(key_parts)
        else:
            arrays.append(value)
        for i, t in enumerate(ts):
            moves.append((len(arrays) - (splits if value is None else 1), i * part, part, t * depth))
    for h in range(1, splits):
        moves.append((h, 0, part, h * part))
    for h, ts, value in key_swaps:
        arrays.append(value)
        for i, t in enumerate(ts):
            moves.append((len(arrays) - 1, i * part, part, t * depth + h * part))
    partial_sums = [None] * group
    for which in [[s, s + 1] for s in reversed(range(0, group, 2))]:
        results = call(
            functools.partial(base_kernel, rows, len(which), tuple(moves), len(arrays)),
            [jax.ShapeDtypeStruct((rows, out_width), f32)] * len(which),
            [VMEM] * len(which),
            [HBM] * (len(which) + len(arrays)),
            [
                pltpu.VMEM((len(which) * rows, held_width), bf16),
                pltpu.VMEM((held_width, out_width), bf16),
                pltpu.SemaphoreType.DMA((2 * len(which) + len(moves),)),
            ],
            2 * len(which) * rows * held_width * out_width,
            2 * held_width * (len(which) * rows + out_width) + 4 * len(which) * rows * out_width,
        )(*[pieces[s] for s in which], *arrays)
        for s, value in zip(which, results):
            partial_sums[s] = value
    bases = layer_sums(partial_sums, True)

    def low_call(bundles, before, last):
        taken = [value for _, value in bundles]
        at = [
            (t, a, i * slots * rank) for a, (ts, _) in enumerate(bundles) for i, t in enumerate(ts)
        ]
        pairs, tall, wide = group // 2, 2 * rows, 2 * local_blocks * rank
        if last:
            outs = [jax.ShapeDtypeStruct((pairs, BLOCK, local_blocks * rank), f32)] * 2
            out_specs = [VMEM] * 2
        else:
            outs, out_specs = jax.ShapeDtypeStruct((pairs, tall, wide), f32), VMEM
        return call(
            functools.partial(
                low_kernel, group, layers, rows, depth, rank, tuple(at), len(taken), by_request,
                shift, before is not None, last,
            ),
            outs,
            out_specs,
            [SMEM] * 3 + [HBM] * (group + len(taken)) + [VMEM] * (before is not None),
            [pltpu.VMEM((group * rows, len(at) * depth), bf16)]
            + [pltpu.VMEM(v.shape, bf16) for v in taken]
            + [pltpu.SemaphoreType.DMA((group, len(at))), pltpu.SemaphoreType.DMA((len(taken),))],
            2 * pairs * tall * wide * len(at) * depth,
            2 * len(at) * depth * (group * rows + slots * rank) + 4 * pairs * tall * wide,
        )(*lists, *pieces, *taken, *([before] if before is not None else []))

    down_bundles[-1] = (down_bundles[-1][0], gate(down_bundles[-1][1], us=30))
    early = low_call([([0], down)] + down_bundles[:-1], None, False)
    even, odd = low_call(down_bundles[-1:], early, True)
    got = swap(odd, "batch", 1)
    lows = layer_pairs(even, got)

    return call(
        functools.partial(final_kernel, rows, rank, len(bases), len(lows)),
        jax.ShapeDtypeStruct((rows, out_width), bf16),
        VMEM,
        [SMEM] * 3 + [VMEM] * (len(bases) + len(lows)) + [HBM],
        [pltpu.VMEM((local_blocks, rank, out_width), bf16), pltpu.SemaphoreType.DMA((local_blocks,))],
        2 * rows * rank * out_width,
        8 * rows * out_width,
    )(*lists, *bases, *lows, adapter_up_factors)


def layer_pairs(mine, got):
    bit = 2
    while mine.shape[0] > 1:
        total = mine + got
        mine, got = total[0::2], swap(total[1::2], "batch", bit)
        bit *= 2
    return [mine[0], got[0]]


def solution(mesh):
    placed = (
        P(("rep", "batch"), None),
        P("batch", None),
        P("batch", None, None),
        P(),
        P("rep"),
        P("rep"),
        P("rep"),
    )
    return jax.shard_map(
        shards, mesh=mesh, in_specs=placed, out_specs=P(("rep", "batch"), None), check_vma=False
    )
```

```python
import functools

import jax
import jax.numpy as jnp
from jax import lax
from jax.experimental import pallas as pl
from jax.experimental.pallas import tpu as pltpu
from jax.sharding import PartitionSpec as P

BLOCK = 128
LANES = 128
MOST = 16
LAYER_CHIPS = 4
VMEM_BYTES = 28 * 1024 * 1024
CORE_FLOPS_PER_US = 1_153_500_000
WAITS = {"far": 12, "keys": 0, "all": 5, "across": 0, "near": 0, "low": (5, 15)}

HBM = pl.BlockSpec(memory_space=pl.ANY)
VMEM = pl.BlockSpec(memory_space=pltpu.VMEM)
SMEM = pl.BlockSpec(memory_space=pltpu.SMEM)


def call(kernel, outs, out_specs, in_specs, scratch, flops, moved):
    return pl.pallas_call(
        kernel,
        out_shape=outs,
        in_specs=in_specs,
        out_specs=out_specs,
        scratch_shapes=scratch,
        compiler_params=pltpu.CompilerParams(vmem_limit_bytes=VMEM_BYTES),
        cost_estimate=pl.CostEstimate(flops=flops, bytes_accessed=moved, transcendentals=0),
    )


def swap(value, axis, bit):
    return lax.ppermute(value, axis, [(i, i ^ bit) for i in range(lax.axis_size(axis))])


def run_copies(pairs, sems):
    copies = [pltpu.make_async_copy(a, b, sems.at[i]) for i, (a, b) in enumerate(pairs)]
    for copy in copies:
        copy.start()
    return copies


def part_start(h, part):
    return pl.multiple_of((lax.axis_index("rep") ^ h) * part, part)


def first_kernel(group, layers, splits, part, key, tokens, *refs):
    keys, refs = refs[:splits], refs[splits:]
    outs, sems = refs[:-1], refs[-1]
    blocks = tokens.shape[0] // BLOCK
    depth = splits * part
    me = lax.axis_index("batch")
    layer, spot = me // group, me % group
    pairs = [(key.at[pl.ds(part_start(h, part), part), :], keys[h]) for h in range(splits)]
    for s in reversed(range(group)):
        for t in range(layers):
            first = ((layer ^ t) * group + (spot ^ s)) * depth
            for h in range(splits):
                start = first + part_start(h, part) if splits > 1 else first
                start = pl.multiple_of(start, part)
                to = pl.ds(t * depth + h * part, part)
                if s < 2:
                    pairs.append((tokens.at[:, pl.ds(start, part)], outs[s].at[:, to]))
                    continue
                for j in range(blocks):
                    pairs.append(
                        (
                            tokens.at[pl.ds(j * BLOCK, BLOCK), pl.ds(start, part)],
                            outs[2 + (s - 2) * blocks + j].at[:, to],
                        )
                    )
    for copy in run_copies(pairs, sems):
        copy.wait()


def stack_kernel(moves, taken, count, *refs):
    values, outs, sems = refs[:taken], refs[count:-1], refs[-1]
    pairs = []
    for o, to, a, row, rows in moves:
        pairs.append((values[a].at[pl.ds(row, rows), :], outs[o].at[pl.ds(to, rows), :]))
    for copy in run_copies(pairs, sems):
        copy.wait()


def stack(lists, *ready, us=0):
    values, moves, outs = [], [], []
    for o, rows_of in enumerate(lists):
        to = 0
        for value, row, rows in rows_of:
            moves.append((o, to, len(values), row, rows))
            values.append(value)
            to += rows
        outs.append(jax.ShapeDtypeStruct((to, value.shape[1]), value.dtype))
    count = len(values) + len(ready)
    return call(
        functools.partial(stack_kernel, tuple(moves), len(values), count),
        outs,
        [VMEM] * len(outs),
        [HBM] * count,
        [pltpu.SemaphoreType.DMA((len(moves),))],
        us * CORE_FLOPS_PER_US,
        0,
    )(*values, *ready)


def gate(value, *ready, us=0):
    return stack([[(value, 0, value.shape[0])]], *ready, us=us)[0]


def chosen_kernel(slots, rank, splits, part, group, layers, shift, picks, down, *refs):
    outs, sems = refs[:-1], refs[-1]
    layer = lax.axis_index("batch") // group
    half = (layer * 2) // layers
    pairs = []
    for n, out in enumerate(outs):
        first = (half ^ 1 ^ n) * shift
        for q in range(slots):
            for h in range(splits):
                start = part_start(h, part) if splits > 1 else 0
                pairs.append(
                    (
                        down.at[picks[first + q], :, pl.ds(start, part)],
                        out.at[pl.ds(q * rank, rank), pl.ds(h * part, part)],
                    )
                )
    for copy in run_copies(pairs, sems):
        copy.wait()


def table(lists, block):
    sizes, adapters, tails = lists
    end = jnp.int32(0)
    owner, adapter, limit = jnp.int32(0), jnp.int32(0), jnp.int32(BLOCK)
    for q in range(sizes.shape[0]):
        begin = end
        end = end + sizes[q]
        inside = (begin <= block) & (block < end)
        owner = jnp.where(inside, q, owner)
        adapter = jnp.where(inside, adapters[q], adapter)
        limit = jnp.where(inside & (block == end - 1), tails[q], limit)
    return owner, adapter, limit


def token_places(group, rows):
    near = [(s * rows, rows) for s in range(min(group, 2))]
    far = [(row, BLOCK) for row in range(2 * rows, group * rows, BLOCK)]
    return near + far


def low_kernel(
    group, layers, rows, depth, rank, entries, count, by_request, shift, has_sum, last, *refs
):
    lists, refs = refs[:3], refs[3:]
    places = token_places(group, rows)
    toks, refs = refs[: len(places)], refs[len(places) :]
    arrays, refs = refs[:count], refs[count:]
    if has_sum:
        before, refs = refs[0], refs[1:]
    if last:
        even, odd, refs = refs[0], refs[1], refs[2:]
    else:
        after, refs = refs[0], refs[1:]
    held, refs = refs[0], refs[1:]
    downs, refs = refs[:count], refs[count:]
    tok_sems, sems = refs
    local_blocks = rows // BLOCK
    me = lax.axis_index("batch")
    layer, spot = me // group, me % group
    first = {}
    started = {}
    for n, (t, a, _) in enumerate(entries):
        if a not in started:
            started[a] = pltpu.make_async_copy(arrays[a], downs[a], sems.at[a])
            started[a].start()
        first[t] = []
        for i, (to, deep) in enumerate(places):
            copy = pltpu.make_async_copy(
                toks[i].at[:, pl.ds(t * depth, depth)],
                held.at[pl.ds(to, deep), pl.ds(n * depth, depth)],
                tok_sems.at[i, n],
            )
            copy.start()
            first[t].append(copy)
    slots = []
    for s in range(group):
        for j in range(local_blocks):
            block = (layer * group + (spot ^ s)) * local_blocks + j
            owner, adapter, _ = table(lists, block)
            slots.append(owner - (layer * 2) // layers * shift if by_request else adapter)
    ready = set()
    wide = 2 * local_blocks
    sums = [before[p] if has_sum else None for p in range(group // 2)]
    for n, (t, a, row) in enumerate(entries):
        for copy in first[t]:
            copy.wait()
        if a not in ready:
            started[a].wait()
            ready.add(a)
        for p in range(group // 2):
            chosen = jnp.concatenate(
                [
                    downs[a][pl.ds(pl.multiple_of(row + slots[p * wide + i] * rank, rank), rank), :]
                    for i in range(wide)
                ],
                0,
            )
            term = lax.dot_general(
                held[2 * p * rows : 2 * (p + 1) * rows, n * depth : (n + 1) * depth],
                chosen,
                (((1,), (1,)), ((), ())),
                preferred_element_type=jnp.float32,
            )
            sums[p] = term if sums[p] is None else sums[p] + term
    for p in range(group // 2):
        if not last:
            after[p] = sums[p]
            continue
        for out, at in ((even, 0), (odd, 1)):
            out[p] = jnp.concatenate(
                [
                    sums[p][
                        (at * local_blocks + j) * BLOCK : (at * local_blocks + j + 1) * BLOCK,
                        (at * local_blocks + j) * rank : (at * local_blocks + j + 1) * rank,
                    ]
                    for j in range(local_blocks)
                ],
                1,
            )


def final_kernel(rows, rank, bases, fars, lows, *refs):
    lists, refs = refs[:3], refs[3:]
    far_refs, refs = refs[:fars], refs[fars:]
    base_refs, refs = refs[:bases], refs[bases:]
    low_refs, refs = refs[:lows], refs[lows:]
    ups, out, up_here, sems = refs
    local_blocks = rows // BLOCK
    me = lax.axis_index("batch")
    found = [table(lists, me * local_blocks + j) for j in range(local_blocks)]
    copies = run_copies([(ups.at[found[j][1]], up_here.at[j]) for j in range(local_blocks)], sems)
    low = low_refs[0][...]
    for ref in low_refs[1:]:
        low = low + ref[...]
    low = low.astype(jnp.bfloat16)
    for j in range(local_blocks):
        copies[j].wait()
        here = pl.ds(j * BLOCK, BLOCK)
        total = jnp.dot(
            low[:, j * rank : (j + 1) * rank], up_here[j], preferred_element_type=jnp.float32
        )
        for ref in base_refs:
            total = total + ref[here, :]
        if far_refs:
            total = total + far_refs[j][...].astype(jnp.float32)
        live = lax.broadcasted_iota(jnp.int32, total.shape, 0) < found[j][2]
        out[here, :] = jnp.where(live, total, 0.0).astype(jnp.bfloat16)


def shards(
    tokens,
    key_matrix,
    adapter_down_factors,
    adapter_up_factors,
    request_block_list,
    request_adapter_index,
    request_tail_tokens,
):
    rows, width = tokens.shape
    depth, out_width = key_matrix.shape
    adapters, rank = adapter_down_factors.shape[1:]
    reps, devices = lax.axis_size("rep"), lax.axis_size("batch")
    group = 2 * LAYER_CHIPS // reps
    layers = devices // group
    splits = reps if (depth // reps) % LANES == 0 else 1
    part = depth // splits
    local_blocks = rows // BLOCK
    held_width = layers * depth
    lists = (request_block_list, request_adapter_index, request_tail_tokens)
    f32, bf16 = jnp.float32, jnp.bfloat16

    far_count = (group - 2) * local_blocks
    first = call(
        functools.partial(first_kernel, group, layers, splits, part),
        [jax.ShapeDtypeStruct((part, out_width), bf16)] * splits
        + [jax.ShapeDtypeStruct((rows, held_width), bf16)] * 2
        + [jax.ShapeDtypeStruct((BLOCK, held_width), bf16)] * far_count,
        [HBM] * (splits + 2 + far_count),
        [HBM] * 2,
        [
            pltpu.SemaphoreType.DMA(
                (splits + (2 + far_count) * layers * splits,)
            )
        ],
        0,
        4 * (rows * width + depth * out_width),
    )(key_matrix, tokens)
    key_parts, first = first[:splits], first[splits:]

    far = [list(first[2 + s * local_blocks :][:local_blocks]) for s in range(group - 2)]
    sent = []
    for j in range(local_blocks if far else 0):
        if j:
            sent = stack([[(f[j], 0, BLOCK)] for f in far], *[f[j - 1] for f in far], us=WAITS["far"])
        else:
            sent = [f[j] for f in far]
        for s, f in enumerate(far):
            f[j] = swap(sent[s], "batch", 2 + s)

    down = jnp.transpose(adapter_down_factors, (1, 2, 0))
    requests = request_adapter_index.shape[0]
    by_request = requests < adapters
    shift = 1 if by_request and local_blocks * devices == 2 * MOST and layers > 1 else 0
    slots = requests - shift if by_request else adapters
    if by_request:
        across, down = call(
            functools.partial(chosen_kernel, slots, rank, splits, part, group, layers, shift),
            [jax.ShapeDtypeStruct((slots * rank, depth), bf16)] * 2,
            [VMEM] * 2,
            [SMEM, HBM],
            [pltpu.SemaphoreType.DMA((2 * slots * splits,))],
            0,
            8 * slots * rank * depth,
        )(request_adapter_index, down)
    else:
        down = down.reshape(slots * rank, depth)
        across = down

    def over_layers(across, near):
        bundles = []
        bit = layers // 2
        while bit:
            moved = [([bit], swap(near if bundles else across, "batch", bit * group))]
            if bundles:
                rest = [v for _, v in bundles]
                rest = rest[0] if len(rest) == 1 else jnp.concatenate(rest, 0)
                order = [t ^ bit for ts, _ in bundles for t in ts]
                moved.append((order, swap(rest, "batch", bit * group)))
            bundles = bundles + moved
            bit //= 2
        return bundles

    key_bundles = over_layers(key_parts[0], key_parts[0])
    rows_of_key = {}
    for h in range(splits):
        rows_of_key[0, h] = (key_parts[h], 0, part)
    for ts, value in key_bundles:
        for i, t in enumerate(ts):
            rows_of_key[t, 0] = (value, i * part, part)
    last_keys = [key_bundles[-1][1]]
    for h in range(1, splits):
        for bundles in (key_bundles[:1], key_bundles[1:]):
            if not bundles:
                continue
            values = bundles[0][1]
            if bundles is not key_bundles[:1] and len(bundles) > 1:
                values = stack([[(v, 0, v.shape[0]) for _, v in bundles]], *last_keys, us=WAITS["keys"])[0]
            last_keys = [values]
            swapped = swap(values, "rep", h)
            if len(bundles) == 1:
                last_keys = [swapped]
            for i, t in enumerate([t for ts, _ in bundles for t in ts]):
                rows_of_key[t, h] = (swapped, i * part, part)
    keys = stack(
        [[rows_of_key[t, h] for t in range(layers) for h in range(splits)]], us=WAITS["all"]
    )[0]

    across_sent = gate(across, *[v for _, v in key_bundles[:2]], us=WAITS["across"])
    down_sent = gate(down, *last_keys, us=WAITS["near"])
    down_bundles = over_layers(across_sent, down_sent)

    near = [first[0], swap(gate(first[1], *[v for _, v in down_bundles[:2]]), "batch", 1)]

    def base_of(value):
        return jnp.dot(value, keys, preferred_element_type=f32)

    fars = []
    if far:
        for j in range(local_blocks):
            theirs = swap(base_of(far[1][j]), "batch", 1)
            fars.append(swap((base_of(far[0][j]) + theirs).astype(bf16), "batch", 2))
    bases = [base_of(near[0]), swap(base_of(near[1]), "batch", 1)]
    tokens_here = near + [value for f in far for value in f]

    def low_call(bundles, before, last):
        taken = [value for _, value in bundles]
        at = [
            (t, a, i * slots * rank) for a, (ts, _) in enumerate(bundles) for i, t in enumerate(ts)
        ]
        pairs, tall, wide = group // 2, 2 * rows, 2 * local_blocks * rank
        if last:
            outs = [jax.ShapeDtypeStruct((pairs, BLOCK, local_blocks * rank), f32)] * 2
            out_specs = [VMEM] * 2
        else:
            outs, out_specs = jax.ShapeDtypeStruct((pairs, tall, wide), f32), VMEM
        return call(
            functools.partial(
                low_kernel, group, layers, rows, depth, rank, tuple(at), len(taken), by_request,
                shift, before is not None, last,
            ),
            outs,
            out_specs,
            [SMEM] * 3 + [HBM] * (len(tokens_here) + len(taken)) + [VMEM] * (before is not None),
            [pltpu.VMEM((group * rows, len(at) * depth), bf16)]
            + [pltpu.VMEM(v.shape, bf16) for v in taken]
            + [pltpu.SemaphoreType.DMA((len(tokens_here), len(at))), pltpu.SemaphoreType.DMA((len(taken),))],
            WAITS["low"][last] * CORE_FLOPS_PER_US,
            0,
        )(*lists, *tokens_here, *taken, *([before] if before is not None else []))

    early = low_call([([0], down)] + down_bundles[:-1], None, False)
    even, odd = low_call(down_bundles[-1:], early, True)
    got = swap(odd, "batch", 1)
    lows = layer_pairs(even, got)

    return call(
        functools.partial(final_kernel, rows, rank, len(bases), len(fars), len(lows)),
        jax.ShapeDtypeStruct((rows, out_width), bf16),
        VMEM,
        [SMEM] * 3 + [VMEM] * (len(fars) + len(bases) + len(lows)) + [HBM],
        [pltpu.VMEM((local_blocks, rank, out_width), bf16), pltpu.SemaphoreType.DMA((local_blocks,))],
        2 * rows * rank * out_width,
        8 * rows * out_width,
    )(*lists, *fars, *bases, *lows, adapter_up_factors)


def layer_pairs(mine, got):
    bit = 2
    while mine.shape[0] > 1:
        total = mine + got
        mine, got = total[0::2], swap(total[1::2], "batch", bit)
        bit *= 2
    return [mine[0], got[0]]


def solution(mesh):
    placed = (
        P(("rep", "batch"), None),
        P("batch", None),
        P("batch", None, None),
        P(),
        P("rep"),
        P("rep"),
        P("rep"),
    )
    return jax.shard_map(
        shards, mesh=mesh, in_specs=placed, out_specs=P(("rep", "batch"), None), check_vma=False
    )
```

```python
import functools

import jax
import jax.numpy as jnp
from jax import lax
from jax.experimental import pallas as pl
from jax.experimental.pallas import tpu as pltpu
from jax.sharding import PartitionSpec as P

BLOCK = 128
LANES = 128
MOST = 16
LAYER_CHIPS = 4
VMEM_BYTES = 28 * 1024 * 1024
CORE_FLOPS_PER_US = 1_153_500_000
WAITS = {"far": 20, "keys": 0, "all": 0, "across": 0, "near": 0, "low": (0, 5)}

HBM = pl.BlockSpec(memory_space=pl.ANY)
VMEM = pl.BlockSpec(memory_space=pltpu.VMEM)
SMEM = pl.BlockSpec(memory_space=pltpu.SMEM)


def call(kernel, outs, out_specs, in_specs, scratch, flops, moved):
    return pl.pallas_call(
        kernel,
        out_shape=outs,
        in_specs=in_specs,
        out_specs=out_specs,
        scratch_shapes=scratch,
        compiler_params=pltpu.CompilerParams(vmem_limit_bytes=VMEM_BYTES),
        cost_estimate=pl.CostEstimate(flops=flops, bytes_accessed=moved, transcendentals=0),
    )


def swap(value, axis, bit):
    return lax.ppermute(value, axis, [(i, i ^ bit) for i in range(lax.axis_size(axis))])


def run_copies(pairs, sems):
    copies = [pltpu.make_async_copy(a, b, sems.at[i]) for i, (a, b) in enumerate(pairs)]
    for copy in copies:
        copy.start()
    return copies


def part_start(h, part):
    return pl.multiple_of((lax.axis_index("rep") ^ h) * part, part)


def key_parts_kernel(splits, part, key, *refs):
    outs, sems = refs[:splits], refs[splits]
    pairs = [(key.at[pl.ds(part_start(h, part), part), :], outs[h]) for h in range(splits)]
    for copy in run_copies(pairs, sems):
        copy.wait()


def token_pieces_kernel(group, layers, splits, part, tokens, *refs):
    outs, sems = refs[:-1], refs[-1]
    blocks = tokens.shape[0] // BLOCK
    depth = splits * part
    me = lax.axis_index("batch")
    layer, spot = me // group, me % group
    pairs = []
    for s in reversed(range(group)):
        for t in range(layers):
            first = ((layer ^ t) * group + (spot ^ s)) * depth
            for h in range(splits):
                start = first + part_start(h, part) if splits > 1 else first
                start = pl.multiple_of(start, part)
                to = pl.ds(t * depth + h * part, part)
                if s < 2:
                    pairs.append((tokens.at[:, pl.ds(start, part)], outs[s].at[:, to]))
                    continue
                for j in range(blocks):
                    pairs.append(
                        (
                            tokens.at[pl.ds(j * BLOCK, BLOCK), pl.ds(start, part)],
                            outs[2 + (s - 2) * blocks + j].at[:, to],
                        )
                    )
    for copy in run_copies(pairs, sems):
        copy.wait()


def stack_kernel(moves, taken, count, *refs):
    values, outs, sems = refs[:taken], refs[count:-1], refs[-1]
    pairs = []
    for o, to, a, row, rows in moves:
        pairs.append((values[a].at[pl.ds(row, rows), :], outs[o].at[pl.ds(to, rows), :]))
    for copy in run_copies(pairs, sems):
        copy.wait()


def stack(lists, *ready, us=0):
    values, moves, outs = [], [], []
    for o, rows_of in enumerate(lists):
        to = 0
        for value, row, rows in rows_of:
            moves.append((o, to, len(values), row, rows))
            values.append(value)
            to += rows
        outs.append(jax.ShapeDtypeStruct((to, value.shape[1]), value.dtype))
    count = len(values) + len(ready)
    return call(
        functools.partial(stack_kernel, tuple(moves), len(values), count),
        outs,
        [VMEM] * len(outs),
        [HBM] * count,
        [pltpu.SemaphoreType.DMA((len(moves),))],
        us * CORE_FLOPS_PER_US,
        0,
    )(*values, *ready)


def gate(value, *ready, us=0):
    return stack([[(value, 0, value.shape[0])]], *ready, us=us)[0]


def chosen_kernel(slots, rank, splits, part, group, layers, shift, picks, down, *refs):
    outs, sems = refs[:-1], refs[-1]
    layer = lax.axis_index("batch") // group
    half = (layer * 2) // layers
    pairs = []
    for n, out in enumerate(outs):
        first = (half ^ 1 ^ n) * shift
        for q in range(slots):
            for h in range(splits):
                start = part_start(h, part) if splits > 1 else 0
                pairs.append(
                    (
                        down.at[picks[first + q], :, pl.ds(start, part)],
                        out.at[pl.ds(q * rank, rank), pl.ds(h * part, part)],
                    )
                )
    for copy in run_copies(pairs, sems):
        copy.wait()


def table(lists, block):
    sizes, adapters, tails = lists
    end = jnp.int32(0)
    owner, adapter, limit = jnp.int32(0), jnp.int32(0), jnp.int32(BLOCK)
    for q in range(sizes.shape[0]):
        begin = end
        end = end + sizes[q]
        inside = (begin <= block) & (block < end)
        owner = jnp.where(inside, q, owner)
        adapter = jnp.where(inside, adapters[q], adapter)
        limit = jnp.where(inside & (block == end - 1), tails[q], limit)
    return owner, adapter, limit


def token_places(group, rows):
    near = [(s * rows, rows) for s in range(min(group, 2))]
    far = [(row, BLOCK) for row in range(2 * rows, group * rows, BLOCK)]
    return near + far


def low_kernel(
    group, layers, rows, depth, rank, entries, count, by_request, shift, has_sum, last, *refs
):
    lists, refs = refs[:3], refs[3:]
    places = token_places(group, rows)
    toks, refs = refs[: len(places)], refs[len(places) :]
    arrays, refs = refs[:count], refs[count:]
    if has_sum:
        before, refs = refs[0], refs[1:]
    if last:
        even, odd, refs = refs[0], refs[1], refs[2:]
    else:
        after, refs = refs[0], refs[1:]
    held, refs = refs[0], refs[1:]
    downs, refs = refs[:count], refs[count:]
    tok_sems, sems = refs
    local_blocks = rows // BLOCK
    me = lax.axis_index("batch")
    layer, spot = me // group, me % group
    first = {}
    started = {}
    for n, (t, a, _) in enumerate(entries):
        if a not in started:
            started[a] = pltpu.make_async_copy(arrays[a], downs[a], sems.at[a])
            started[a].start()
        first[t] = []
        for i, (to, deep) in enumerate(places):
            copy = pltpu.make_async_copy(
                toks[i].at[:, pl.ds(t * depth, depth)],
                held.at[pl.ds(to, deep), pl.ds(n * depth, depth)],
                tok_sems.at[i, n],
            )
            copy.start()
            first[t].append(copy)
    slots = []
    for s in range(group):
        for j in range(local_blocks):
            block = (layer * group + (spot ^ s)) * local_blocks + j
            owner, adapter, _ = table(lists, block)
            slots.append(owner - (layer * 2) // layers * shift if by_request else adapter)
    ready = set()
    wide = 2 * local_blocks
    sums = [before[p] if has_sum else None for p in range(group // 2)]
    for n, (t, a, row) in enumerate(entries):
        for copy in first[t]:
            copy.wait()
        if a not in ready:
            started[a].wait()
            ready.add(a)
        for p in range(group // 2):
            chosen = jnp.concatenate(
                [
                    downs[a][pl.ds(pl.multiple_of(row + slots[p * wide + i] * rank, rank), rank), :]
                    for i in range(wide)
                ],
                0,
            )
            term = lax.dot_general(
                held[2 * p * rows : 2 * (p + 1) * rows, n * depth : (n + 1) * depth],
                chosen,
                (((1,), (1,)), ((), ())),
                preferred_element_type=jnp.float32,
            )
            sums[p] = term if sums[p] is None else sums[p] + term
    for p in range(group // 2):
        if not last:
            after[p] = sums[p]
            continue
        for out, at in ((even, 0), (odd, 1)):
            out[p] = jnp.concatenate(
                [
                    sums[p][
                        (at * local_blocks + j) * BLOCK : (at * local_blocks + j + 1) * BLOCK,
                        (at * local_blocks + j) * rank : (at * local_blocks + j + 1) * rank,
                    ]
                    for j in range(local_blocks)
                ],
                1,
            )


def final_kernel(rows, rank, bases, fars, lows, *refs):
    lists, refs = refs[:3], refs[3:]
    far_refs, refs = refs[:fars], refs[fars:]
    base_refs, refs = refs[:bases], refs[bases:]
    low_refs, refs = refs[:lows], refs[lows:]
    ups, out, up_here, sems = refs
    local_blocks = rows // BLOCK
    me = lax.axis_index("batch")
    found = [table(lists, me * local_blocks + j) for j in range(local_blocks)]
    copies = run_copies([(ups.at[found[j][1]], up_here.at[j]) for j in range(local_blocks)], sems)
    low = low_refs[0][...]
    for ref in low_refs[1:]:
        low = low + ref[...]
    low = low.astype(jnp.bfloat16)
    for j in range(local_blocks):
        copies[j].wait()
        here = pl.ds(j * BLOCK, BLOCK)
        total = jnp.dot(
            low[:, j * rank : (j + 1) * rank], up_here[j], preferred_element_type=jnp.float32
        )
        for ref in base_refs:
            total = total + ref[here, :]
        if far_refs:
            total = total + far_refs[0][here, :].astype(jnp.float32)
        live = lax.broadcasted_iota(jnp.int32, total.shape, 0) < found[j][2]
        out[here, :] = jnp.where(live, total, 0.0).astype(jnp.bfloat16)


def shards(
    tokens,
    key_matrix,
    adapter_down_factors,
    adapter_up_factors,
    request_block_list,
    request_adapter_index,
    request_tail_tokens,
):
    rows, width = tokens.shape
    depth, out_width = key_matrix.shape
    adapters, rank = adapter_down_factors.shape[1:]
    reps, devices = lax.axis_size("rep"), lax.axis_size("batch")
    group = 2 * LAYER_CHIPS // reps
    layers = devices // group
    splits = reps if (depth // reps) % LANES == 0 else 1
    part = depth // splits
    local_blocks = rows // BLOCK
    held_width = layers * depth
    lists = (request_block_list, request_adapter_index, request_tail_tokens)
    f32, bf16 = jnp.float32, jnp.bfloat16

    if splits > 1:
        key_parts = call(
            functools.partial(key_parts_kernel, splits, part),
            [jax.ShapeDtypeStruct((part, out_width), bf16)] * splits,
            [HBM] * splits,
            [HBM],
            [pltpu.SemaphoreType.DMA((splits,))],
            0,
            4 * depth * out_width,
        )(key_matrix)
    else:
        key_parts = [key_matrix]
    far_count = (group - 2) * local_blocks
    first = call(
        functools.partial(token_pieces_kernel, group, layers, splits, part),
        [jax.ShapeDtypeStruct((rows, held_width), bf16)] * 2
        + [jax.ShapeDtypeStruct((BLOCK, held_width), bf16)] * far_count,
        [HBM] * (2 + far_count),
        [HBM],
        [pltpu.SemaphoreType.DMA(((2 + far_count * local_blocks) * layers * splits,))],
        0,
        4 * rows * width,
    )(tokens)

    near = [first[0], swap(first[1], "batch", 1)]
    far = [list(first[2 + s * local_blocks :][:local_blocks]) for s in range(group - 2)]
    sent = []
    for j in range(local_blocks if far else 0):
        if j:
            sent = stack([[(f[j], 0, BLOCK)] for f in far], *[f[j - 1] for f in far], us=WAITS["far"])
        else:
            sent = [f[j] for f in far]
        for s, f in enumerate(far):
            f[j] = swap(sent[s], "batch", 2 + s)

    down = jnp.transpose(adapter_down_factors, (1, 2, 0))
    requests = request_adapter_index.shape[0]
    by_request = requests < adapters
    shift = 1 if by_request and local_blocks * devices == 2 * MOST and layers == 4 else 0
    slots = requests - shift if by_request else adapters
    if by_request:
        across, down = call(
            functools.partial(chosen_kernel, slots, rank, splits, part, group, layers, shift),
            [jax.ShapeDtypeStruct((slots * rank, depth), bf16)] * 2,
            [VMEM] * 2,
            [SMEM, HBM],
            [pltpu.SemaphoreType.DMA((2 * slots * splits,))],
            0,
            8 * slots * rank * depth,
        )(request_adapter_index, down)
    else:
        down = down.reshape(slots * rank, depth)
        across = down

    def over_layers(own):
        bundles = []
        bit = layers // 2
        while bit:
            moved = [([bit], swap(own, "batch", bit * group))]
            if bundles:
                rest = [v for _, v in bundles]
                rest = rest[0] if len(rest) == 1 else jnp.concatenate(rest, 0)
                order = [t ^ bit for ts, _ in bundles for t in ts]
                moved.append((order, swap(rest, "batch", bit * group)))
            bundles = bundles + moved
            bit //= 2
        return bundles

    key_bundles = over_layers(key_parts[0])
    rows_of_key = {}
    for h in range(splits):
        rows_of_key[0, h] = (key_parts[h], 0, part)
    for ts, value in key_bundles:
        for i, t in enumerate(ts):
            rows_of_key[t, 0] = (value, i * part, part)
    last_keys = [key_bundles[-1][1]]
    for h in range(1, splits):
        for bundles in (key_bundles[:2], key_bundles[2:]):
            if not bundles:
                continue
            if bundles[0] is key_bundles[0]:
                values = stack([[(v, 0, v.shape[0]) for _, v in bundles]], near[1])[0]
                swapped = swap(values, "rep", h)
            else:
                values = stack([[(v, 0, v.shape[0]) for _, v in bundles]], swapped, *sent, us=WAITS["keys"])[0]
                swapped = swap(values, "rep", h)
                last_keys = [values]
            for i, t in enumerate([t for ts, _ in bundles for t in ts]):
                rows_of_key[t, h] = (swapped, i * part, part)
    keys = stack(
        [[rows_of_key[t, h] for t in range(layers) for h in range(splits)]], us=WAITS["all"]
    )[0]

    if layers == 4:
        got = {}
        got[2] = swap(gate(across, *[v for _, v in key_bundles[:2]], us=WAITS["across"]), "batch", 2 * group)
        sent_last = gate(across, *last_keys, us=WAITS["near"])
        got[3] = swap(sent_last, "batch", 3 * group)
        sent_near = gate(down, got[2], sent_last)
        got[1] = swap(sent_near, "batch", group)
        down_bundles = [([t], got[t]) for t in (2, 1, 3)]
    else:
        down_bundles = over_layers(down)

    def base_of(value):
        return jnp.dot(value, keys, preferred_element_type=f32)

    fars = []
    if far:
        sums = []
        for j in range(local_blocks):
            theirs = swap(base_of(far[1][j]), "batch", 1)
            sums.append((base_of(far[0][j]) + theirs).astype(bf16))
        fars = [swap(jnp.concatenate(sums, 0), "batch", 2)]
    bases = [base_of(near[0]), swap(base_of(near[1]), "batch", 1)]
    tokens_here = near + [value for f in far for value in f]

    def low_call(bundles, before, last):
        taken = [value for _, value in bundles]
        at = [
            (t, a, i * slots * rank) for a, (ts, _) in enumerate(bundles) for i, t in enumerate(ts)
        ]
        pairs, tall, wide = group // 2, 2 * rows, 2 * local_blocks * rank
        if last:
            outs = [jax.ShapeDtypeStruct((pairs, BLOCK, local_blocks * rank), f32)] * 2
            out_specs = [VMEM] * 2
        else:
            outs, out_specs = jax.ShapeDtypeStruct((pairs, tall, wide), f32), VMEM
        return call(
            functools.partial(
                low_kernel, group, layers, rows, depth, rank, tuple(at), len(taken), by_request,
                shift, before is not None, last,
            ),
            outs,
            out_specs,
            [SMEM] * 3 + [HBM] * (len(tokens_here) + len(taken)) + [VMEM] * (before is not None),
            [pltpu.VMEM((group * rows, len(at) * depth), bf16)]
            + [pltpu.VMEM(v.shape, bf16) for v in taken]
            + [pltpu.SemaphoreType.DMA((len(tokens_here), len(at))), pltpu.SemaphoreType.DMA((len(taken),))],
            WAITS["low"][last] * CORE_FLOPS_PER_US,
            0,
        )(*lists, *tokens_here, *taken, *([before] if before is not None else []))

    early = low_call([([0], down)] + down_bundles[:-1], None, False)
    even, odd = low_call(down_bundles[-1:], early, True)
    got = swap(odd, "batch", 1)
    lows = layer_pairs(even, got)

    return call(
        functools.partial(final_kernel, rows, rank, len(bases), len(fars), len(lows)),
        jax.ShapeDtypeStruct((rows, out_width), bf16),
        VMEM,
        [SMEM] * 3 + [VMEM] * (len(fars) + len(bases) + len(lows)) + [HBM],
        [pltpu.VMEM((local_blocks, rank, out_width), bf16), pltpu.SemaphoreType.DMA((local_blocks,))],
        2 * rows * rank * out_width,
        8 * rows * out_width,
    )(*lists, *fars, *bases, *lows, adapter_up_factors)


def layer_pairs(mine, got):
    bit = 2
    while mine.shape[0] > 1:
        total = mine + got
        mine, got = total[0::2], swap(total[1::2], "batch", bit)
        bit *= 2
    return [mine[0], got[0]]


def solution(mesh):
    placed = (
        P(("rep", "batch"), None),
        P("batch", None),
        P("batch", None, None),
        P(),
        P("rep"),
        P("rep"),
        P("rep"),
    )
    return jax.shard_map(
        shards, mesh=mesh, in_specs=placed, out_specs=P(("rep", "batch"), None), check_vma=False
    )
```

```python
import functools

import jax
import jax.numpy as jnp
from jax import lax
from jax.experimental import pallas as pl
from jax.experimental.pallas import tpu as pltpu
from jax.sharding import PartitionSpec as P

BLOCK = 128
LANES = 128
MOST = 16
LAYER_CHIPS = 4
VMEM_BYTES = 28 * 1024 * 1024
CORE_FLOPS_PER_US = 1_153_500_000
PHASES = (7, 6, 3)

HBM = pl.BlockSpec(memory_space=pl.ANY)
VMEM = pl.BlockSpec(memory_space=pltpu.VMEM)
SMEM = pl.BlockSpec(memory_space=pltpu.SMEM)


def call(kernel, outs, out_specs, in_specs, scratch, flops, moved):
    return pl.pallas_call(
        kernel,
        out_shape=outs,
        in_specs=in_specs,
        out_specs=out_specs,
        scratch_shapes=scratch,
        compiler_params=pltpu.CompilerParams(vmem_limit_bytes=VMEM_BYTES),
        cost_estimate=pl.CostEstimate(flops=flops, bytes_accessed=moved, transcendentals=0),
    )


def swap(value, axis, bit):
    return lax.ppermute(value, axis, [(i, i ^ bit) for i in range(lax.axis_size(axis))])


def run_copies(pairs, sems):
    copies = [pltpu.make_async_copy(a, b, sems.at[i]) for i, (a, b) in enumerate(pairs)]
    for copy in copies:
        copy.start()
    return copies


def part_start(h, part):
    return pl.multiple_of((lax.axis_index("rep") ^ h) * part, part)


def key_parts_kernel(splits, part, key, *refs):
    outs, sems = refs[:splits], refs[splits]
    pairs = [(key.at[pl.ds(part_start(h, part), part), :], outs[h]) for h in range(splits)]
    for copy in run_copies(pairs, sems):
        copy.wait()


def token_pieces_kernel(group, layers, splits, part, chunks, tokens, *refs):
    outs, sems = refs[:-1], refs[-1]
    depth = splits * part
    me = lax.axis_index("batch")
    layer, spot = me // group, me % group
    pairs = []
    for s in reversed(range(group)):
        for t in range(layers):
            first = ((layer ^ t) * group + (spot ^ s)) * depth
            for h in range(splits):
                start = first + part_start(h, part) if splits > 1 else first
                start = pl.multiple_of(start, part)
                to = pl.ds(t * depth + h * part, part)
                if s < 2:
                    pairs.append((tokens.at[:, pl.ds(start, part)], outs[s].at[:, to]))
                    continue
                for i, (row, deep) in enumerate(chunks):
                    pairs.append(
                        (
                            tokens.at[pl.ds(row, deep), pl.ds(start, part)],
                            outs[2 + (s - 2) * len(chunks) + i].at[:, to],
                        )
                    )
    for copy in run_copies(pairs, sems):
        copy.wait()


def stack_kernel(moves, taken, count, *refs):
    values, outs, sems = refs[:taken], refs[count:-1], refs[-1]
    pairs = []
    for o, to, a, row, rows in moves:
        pairs.append((values[a].at[pl.ds(row, rows), :], outs[o].at[pl.ds(to, rows), :]))
    for copy in run_copies(pairs, sems):
        copy.wait()


def stack(lists, *ready, us=0):
    values, moves, outs = [], [], []
    for o, rows_of in enumerate(lists):
        to = 0
        for value, row, rows in rows_of:
            moves.append((o, to, len(values), row, rows))
            values.append(value)
            to += rows
        outs.append(jax.ShapeDtypeStruct((to, value.shape[1]), value.dtype))
    count = len(values) + len(ready)
    return call(
        functools.partial(stack_kernel, tuple(moves), len(values), count),
        outs,
        [VMEM] * len(outs),
        [HBM] * count,
        [pltpu.SemaphoreType.DMA((len(moves),))],
        us * CORE_FLOPS_PER_US,
        0,
    )(*values, *ready)


def gate(value, *ready, us=0):
    return stack([[(value, 0, value.shape[0])]], *ready, us=us)[0]


def chosen_kernel(slots, rank, splits, part, group, layers, shift, picks, down, *refs):
    outs, sems = refs[:-1], refs[-1]
    layer = lax.axis_index("batch") // group
    half = (layer * 2) // layers
    pairs = []
    for n, out in enumerate(outs):
        first = (half ^ 1 ^ n) * shift
        for q in range(slots):
            for h in range(splits):
                start = part_start(h, part) if splits > 1 else 0
                pairs.append(
                    (
                        down.at[picks[first + q], :, pl.ds(start, part)],
                        out.at[pl.ds(q * rank, rank), pl.ds(h * part, part)],
                    )
                )
    for copy in run_copies(pairs, sems):
        copy.wait()


def table(lists, block):
    sizes, adapters, tails = lists
    end = jnp.int32(0)
    owner, adapter, limit = jnp.int32(0), jnp.int32(0), jnp.int32(BLOCK)
    for q in range(sizes.shape[0]):
        begin = end
        end = end + sizes[q]
        inside = (begin <= block) & (block < end)
        owner = jnp.where(inside, q, owner)
        adapter = jnp.where(inside, adapters[q], adapter)
        limit = jnp.where(inside & (block == end - 1), tails[q], limit)
    return owner, adapter, limit


def low_kernel(
    group, layers, rows, depth, rank, entries, count, by_request, shift, has_sum, last, *refs
):
    lists, refs = refs[:3], refs[3:]
    toks, refs = refs[:group], refs[group:]
    arrays, refs = refs[: len(count)], refs[len(count) :]
    if has_sum:
        before, refs = refs[0], refs[1:]
    if last:
        even, odd, refs = refs[0], refs[1], refs[2:]
    else:
        after, refs = refs[0], refs[1:]
    held, refs = refs[0], refs[1:]
    buffers = count[-1][0] + 1
    downs, refs = refs[:buffers], refs[buffers:]
    tok_sems, sems = refs
    local_blocks = rows // BLOCK
    me = lax.axis_index("batch")
    layer, spot = me // group, me % group
    first = {}
    started = {}
    for n, (t, a, _) in enumerate(entries):
        if a not in started:
            started[a], to = [], 0
            for i, (buffer, tall) in enumerate(count):
                if buffer != a:
                    continue
                copy = pltpu.make_async_copy(arrays[i], downs[a].at[pl.ds(to, tall), :], sems.at[i])
                copy.start()
                started[a].append(copy)
                to += tall
        first[t] = []
        for s in range(group):
            copy = pltpu.make_async_copy(
                toks[s].at[:, pl.ds(t * depth, depth)],
                held.at[pl.ds(s * rows, rows), pl.ds(n * depth, depth)],
                tok_sems.at[s, n],
            )
            copy.start()
            first[t].append(copy)
    slots = []
    for s in range(group):
        for j in range(local_blocks):
            block = (layer * group + (spot ^ s)) * local_blocks + j
            owner, adapter, _ = table(lists, block)
            slots.append(owner - (layer * 2) // layers * shift if by_request else adapter)
    ready = set()
    wide = 2 * local_blocks
    sums = [before[p] if has_sum else None for p in range(group // 2)]
    for n, (t, a, row) in enumerate(entries):
        for copy in first[t]:
            copy.wait()
        if a not in ready:
            for copy in started[a]:
                copy.wait()
            ready.add(a)
        for p in range(group // 2):
            chosen = jnp.concatenate(
                [
                    downs[a][pl.ds(pl.multiple_of(row + slots[p * wide + i] * rank, rank), rank), :]
                    for i in range(wide)
                ],
                0,
            )
            term = lax.dot_general(
                held[2 * p * rows : 2 * (p + 1) * rows, n * depth : (n + 1) * depth],
                chosen,
                (((1,), (1,)), ((), ())),
                preferred_element_type=jnp.float32,
            )
            sums[p] = term if sums[p] is None else sums[p] + term
    for p in range(group // 2):
        if not last:
            after[p] = sums[p]
            continue
        for out, at in ((even, 0), (odd, 1)):
            out[p] = jnp.concatenate(
                [
                    sums[p][
                        (at * local_blocks + j) * BLOCK : (at * local_blocks + j + 1) * BLOCK,
                        (at * local_blocks + j) * rank : (at * local_blocks + j + 1) * rank,
                    ]
                    for j in range(local_blocks)
                ],
                1,
            )


def final_kernel(rows, rank, bases, fars, lows, *refs):
    lists, refs = refs[:3], refs[3:]
    far_refs, refs = refs[:fars], refs[fars:]
    base_refs, refs = refs[:bases], refs[bases:]
    low_refs, refs = refs[:lows], refs[lows:]
    ups, out, up_here, sems = refs
    local_blocks = rows // BLOCK
    me = lax.axis_index("batch")
    found = [table(lists, me * local_blocks + j) for j in range(local_blocks)]
    copies = run_copies([(ups.at[found[j][1]], up_here.at[j]) for j in range(local_blocks)], sems)
    low = low_refs[0][...]
    for ref in low_refs[1:]:
        low = low + ref[...]
    low = low.astype(jnp.bfloat16)
    for j in range(local_blocks):
        copies[j].wait()
        here = pl.ds(j * BLOCK, BLOCK)
        total = jnp.dot(
            low[:, j * rank : (j + 1) * rank], up_here[j], preferred_element_type=jnp.float32
        )
        for ref in base_refs:
            total = total + ref[here, :]
        if far_refs:
            total = total + far_refs[j][...].astype(jnp.float32)
        live = lax.broadcasted_iota(jnp.int32, total.shape, 0) < found[j][2]
        out[here, :] = jnp.where(live, total, 0.0).astype(jnp.bfloat16)


def shards(
    tokens,
    key_matrix,
    adapter_down_factors,
    adapter_up_factors,
    request_block_list,
    request_adapter_index,
    request_tail_tokens,
):
    rows, width = tokens.shape
    depth, out_width = key_matrix.shape
    adapters, rank = adapter_down_factors.shape[1:]
    reps, devices = lax.axis_size("rep"), lax.axis_size("batch")
    group = 2 * LAYER_CHIPS // reps
    layers = devices // group
    splits = reps if (depth // reps) % LANES == 0 else 1
    part = depth // splits
    local_blocks = rows // BLOCK
    held_width = layers * depth
    lists = (request_block_list, request_adapter_index, request_tail_tokens)
    f32, bf16 = jnp.float32, jnp.bfloat16

    if splits > 1:
        key_parts = call(
            functools.partial(key_parts_kernel, splits, part),
            [jax.ShapeDtypeStruct((part, out_width), bf16)] * splits,
            [HBM] * splits,
            [HBM],
            [pltpu.SemaphoreType.DMA((splits,))],
            0,
            4 * depth * out_width,
        )(key_matrix)
    else:
        key_parts = [key_matrix]
    chunks = [
        (sum(PHASES[:i]) * rows // sum(PHASES), PHASES[i] * rows // sum(PHASES))
        for i in range(len(PHASES) if group > 2 else 0)
    ]
    cut = call(
        functools.partial(token_pieces_kernel, group, layers, splits, part, chunks),
        [jax.ShapeDtypeStruct((rows, held_width), bf16)] * 2
        + [jax.ShapeDtypeStruct((deep, held_width), bf16) for _, deep in chunks] * (group - 2),
        [HBM] * (2 + (group - 2) * len(chunks)),
        [HBM],
        [pltpu.SemaphoreType.DMA(((2 + (group - 2) * len(chunks)) * layers * splits,))],
        0,
        4 * rows * width,
    )(tokens)
    far = [list(cut[2 + s * len(chunks) :][: len(chunks)]) for s in range(group - 2)]

    def cross(i, values):
        for s, value in enumerate(values):
            far[s][i] = swap(value, "batch", 2 + s)
        return [f[i] for f in far]

    def whole(value):
        return [(value, 0, value.shape[0])]

    down = jnp.transpose(adapter_down_factors, (1, 2, 0))
    requests = request_adapter_index.shape[0]
    by_request = requests < adapters
    shift = 1 if by_request and local_blocks * devices == 2 * MOST and far and splits == 2 and layers == 4 else 0
    slots = requests - shift if by_request else adapters
    if by_request:
        across, down = call(
            functools.partial(chosen_kernel, slots, rank, splits, part, group, layers, shift),
            [jax.ShapeDtypeStruct((slots * rank, depth), bf16)] * 2,
            [VMEM] * 2,
            [SMEM, HBM],
            [pltpu.SemaphoreType.DMA((2 * slots * splits,))],
            0,
            8 * slots * rank * depth,
        )(request_adapter_index, down)
    else:
        down = down.reshape(slots * rank, depth)
        across = down

    def over_layers(own):
        bundles = []
        bit = layers // 2
        while bit:
            moved = [([bit], swap(own, "batch", bit * group))]
            if bundles:
                rest = [v for _, v in bundles]
                rest = rest[0] if len(rest) == 1 else jnp.concatenate(rest, 0)
                order = [t ^ bit for ts, _ in bundles for t in ts]
                moved.append((order, swap(rest, "batch", bit * group)))
            bundles = bundles + moved
            bit //= 2
        return bundles

    rows_of_key = {}
    for h in range(splits):
        rows_of_key[0, h] = (key_parts[h], 0, part)
    other = swap(cut[1], "batch", 1)
    if layers == 4 and splits == 2 and far:
        keys_far = swap(key_parts[0], "batch", 2 * group)
        keys_near = swap(key_parts[0], "batch", group)
        tokens_here = cross(0, [f[0] for f in far])
        opened = stack(
            [whole(keys_far) + whole(keys_near), whole(across)] + [whole(f[1]) for f in far],
            other,
            *tokens_here,
        )
        keys_last = swap(keys_far, "batch", group)
        halves = swap(opened[0], "rep", 1)
        downs_far = swap(opened[1], "batch", 2 * group)
        tokens_here = cross(1, opened[2:])
        cut_at = (slots + 1) // 2 * rank
        parts_of = [(0, cut_at), (cut_at, slots * rank - cut_at)]
        opened = stack(
            [[(v, *parts_of[0])] for v in (across, down)] + [whole(f[2]) for f in far],
            keys_last,
            halves,
            downs_far,
            *tokens_here,
        )
        downs_last = [swap(opened[0], "batch", 3 * group)]
        downs_near = [swap(opened[1], "batch", group)]
        cross(2, opened[2:])
        halves_last = swap(keys_last, "rep", 1)
        rows_of_key[2, 0], rows_of_key[1, 0] = whole(keys_far)[0], whole(keys_near)[0]
        rows_of_key[3, 0], rows_of_key[3, 1] = whole(keys_last)[0], whole(halves_last)[0]
        rows_of_key[2, 1], rows_of_key[1, 1] = (halves, 0, part), (halves, part, part)
        opened = stack(
            [[(v, *parts_of[1])] for v in (across, down)]
            + [[rows_of_key[t, h] for t in range(layers) for h in range(splits)]]
            + [sum([whole(value) for value in f], []) for f in far],
            downs_last[0],
            downs_near[0],
        )
        downs_last.append(swap(opened[0], "batch", 3 * group))
        downs_near.append(swap(opened[1], "batch", group))
        keys, pieces = opened[2], [cut[0], other, *opened[3:]]
        down_bundles = [([2], [downs_far]), ([1], downs_near), ([3], downs_last)]
    else:
        for f in range(len(chunks)):
            cross(f, [values[f] for values in far])
        for ts, value in over_layers(key_parts[0]):
            for i, t in enumerate(ts):
                rows_of_key[t, 0] = (value, i * part, part)
            for h in range(1, splits):
                swapped = swap(value, "rep", h)
                for i, t in enumerate(ts):
                    rows_of_key[t, h] = (swapped, i * part, part)
        down_bundles = [(ts, [value]) for ts, value in over_layers(down)]
        keys = stack([[rows_of_key[t, h] for t in range(layers) for h in range(splits)]])[0]
        pieces = [cut[0], other]
        if far:
            pieces += stack([sum([whole(value) for value in f], []) for f in far])

    def base_of(value):
        return jnp.dot(value, keys, preferred_element_type=f32)

    parts = [base_of(value) for value in pieces]
    bases = [parts[0], swap(parts[1], "batch", 1)]
    fars = []
    if group > 2:
        theirs = swap(parts[3], "batch", 1)
        for j in range(local_blocks):
            here = slice(j * BLOCK, (j + 1) * BLOCK)
            fars.append(swap((parts[2][here] + theirs[here]).astype(bf16), "batch", 2))
        order, values = down_bundles[-1]
        down_bundles[-1] = (order, values[:-1] + [gate(values[-1], fars[0])])

    def low_call(bundles, before, last):
        taken = [value for _, values in bundles for value in values]
        count = tuple((a, v.shape[0]) for a, (_, values) in enumerate(bundles) for v in values)
        at = [
            (t, a, i * slots * rank) for a, (ts, _) in enumerate(bundles) for i, t in enumerate(ts)
        ]
        pairs, tall, wide = group // 2, 2 * rows, 2 * local_blocks * rank
        if last:
            outs = [jax.ShapeDtypeStruct((pairs, BLOCK, local_blocks * rank), f32)] * 2
            out_specs = [VMEM] * 2
        else:
            outs, out_specs = jax.ShapeDtypeStruct((pairs, tall, wide), f32), VMEM
        return call(
            functools.partial(
                low_kernel, group, layers, rows, depth, rank, tuple(at), count, by_request,
                shift, before is not None, last,
            ),
            outs,
            out_specs,
            [SMEM] * 3 + [HBM] * (len(pieces) + len(taken)) + [VMEM] * (before is not None),
            [pltpu.VMEM((group * rows, len(at) * depth), bf16)]
            + [
                pltpu.VMEM((sum(v.shape[0] for v in values), depth), bf16) for _, values in bundles
            ]
            + [pltpu.SemaphoreType.DMA((len(pieces), len(at))), pltpu.SemaphoreType.DMA((len(taken),))],
            2 * pairs * tall * wide * len(at) * depth,
            2 * len(at) * depth * (group * rows + slots * rank) + 4 * pairs * tall * wide,
        )(*lists, *pieces, *taken, *([before] if before is not None else []))

    early = low_call([([0], [down])] + down_bundles[:-1], None, False)
    even, odd = low_call(down_bundles[-1:], early, True)
    got = swap(odd, "batch", 1)
    lows = layer_pairs(even, got)

    return call(
        functools.partial(final_kernel, rows, rank, len(bases), len(fars), len(lows)),
        jax.ShapeDtypeStruct((rows, out_width), bf16),
        VMEM,
        [SMEM] * 3 + [VMEM] * (len(fars) + len(bases) + len(lows)) + [HBM],
        [pltpu.VMEM((local_blocks, rank, out_width), bf16), pltpu.SemaphoreType.DMA((local_blocks,))],
        2 * rows * rank * out_width,
        8 * rows * out_width,
    )(*lists, *fars, *bases, *lows, adapter_up_factors)


def layer_pairs(mine, got):
    bit = 2
    while mine.shape[0] > 1:
        total = mine + got
        mine, got = total[0::2], swap(total[1::2], "batch", bit)
        bit *= 2
    return [mine[0], got[0]]


def solution(mesh):
    placed = (
        P(("rep", "batch"), None),
        P("batch", None),
        P("batch", None, None),
        P(),
        P("rep"),
        P("rep"),
        P("rep"),
    )
    return jax.shard_map(
        shards, mesh=mesh, in_specs=placed, out_specs=P(("rep", "batch"), None), check_vma=False
    )
```

```python
import functools

import jax
import jax.numpy as jnp
from jax import lax
from jax.experimental import pallas as pl
from jax.experimental.pallas import tpu as pltpu
from jax.sharding import PartitionSpec as P

BLOCK = 128
LANES = 128
MOST = 16
LAYER_CHIPS = 4
VMEM_BYTES = 28 * 1024 * 1024
CORE_FLOPS_PER_US = 1_153_500_000
CFG = {'us': {}, 'z3': 2, 'c': 2, 'xcut': 2, 'ph': [11, 5]}
WAITS = {"far": 12, "keys": 0, "all": 5, "across": 0, "near": 0, "low": (5, 15)}
WAITS.update(CFG.get("us", {}))
PHASES = tuple(CFG.get("ph", [8, 8]))

HBM = pl.BlockSpec(memory_space=pl.ANY)
VMEM = pl.BlockSpec(memory_space=pltpu.VMEM)
SMEM = pl.BlockSpec(memory_space=pltpu.SMEM)


def call(kernel, outs, out_specs, in_specs, scratch, flops, moved):
    return pl.pallas_call(
        kernel,
        out_shape=outs,
        in_specs=in_specs,
        out_specs=out_specs,
        scratch_shapes=scratch,
        compiler_params=pltpu.CompilerParams(vmem_limit_bytes=VMEM_BYTES),
        cost_estimate=pl.CostEstimate(flops=flops, bytes_accessed=moved, transcendentals=0),
    )


def swap(value, axis, bit):
    return lax.ppermute(value, axis, [(i, i ^ bit) for i in range(lax.axis_size(axis))])


def run_copies(pairs, sems):
    copies = [pltpu.make_async_copy(a, b, sems.at[i]) for i, (a, b) in enumerate(pairs)]
    for copy in copies:
        copy.start()
    return copies


def part_start(h, part):
    return pl.multiple_of((lax.axis_index("rep") ^ h) * part, part)


def first_kernel(group, layers, splits, part, chunks, key, tokens, *refs):
    keys, refs = refs[:splits], refs[splits:]
    outs, sems = refs[:-1], refs[-1]
    depth = splits * part
    me = lax.axis_index("batch")
    layer, spot = me // group, me % group
    pairs = [(key.at[pl.ds(part_start(h, part), part), :], keys[h]) for h in range(splits)]
    for s in reversed(range(group)):
        for t in range(layers):
            first = ((layer ^ t) * group + (spot ^ s)) * depth
            for h in range(splits):
                start = first + part_start(h, part) if splits > 1 else first
                start = pl.multiple_of(start, part)
                to = pl.ds(t * depth + h * part, part)
                if s < 2:
                    pairs.append((tokens.at[:, pl.ds(start, part)], outs[s].at[:, to]))
                    continue
                for j, (row, deep) in enumerate(chunks):
                    pairs.append(
                        (
                            tokens.at[pl.ds(row, deep), pl.ds(start, part)],
                            outs[2 + (s - 2) * len(chunks) + j].at[:, to],
                        )
                    )
    for copy in run_copies(pairs, sems):
        copy.wait()


def stack_kernel(moves, taken, count, *refs):
    values, outs, sems = refs[:taken], refs[count:-1], refs[-1]
    pairs = []
    for o, to, a, row, rows in moves:
        pairs.append((values[a].at[pl.ds(row, rows), :], outs[o].at[pl.ds(to, rows), :]))
    for copy in run_copies(pairs, sems):
        copy.wait()


def stack(lists, *ready, us=0):
    values, moves, outs = [], [], []
    for o, rows_of in enumerate(lists):
        to = 0
        for value, row, rows in rows_of:
            moves.append((o, to, len(values), row, rows))
            values.append(value)
            to += rows
        outs.append(jax.ShapeDtypeStruct((to, value.shape[1]), value.dtype))
    count = len(values) + len(ready)
    return call(
        functools.partial(stack_kernel, tuple(moves), len(values), count),
        outs,
        [VMEM] * len(outs),
        [HBM] * count,
        [pltpu.SemaphoreType.DMA((len(moves),))],
        us * CORE_FLOPS_PER_US,
        0,
    )(*values, *ready)


def gate(value, *ready, us=0):
    return stack([[(value, 0, value.shape[0])]], *ready, us=us)[0]


def chosen_kernel(slots, rank, splits, part, group, layers, shift, picks, down, *refs):
    outs, sems = refs[:-1], refs[-1]
    layer = lax.axis_index("batch") // group
    half = (layer * 2) // layers
    pairs = []
    for n, out in enumerate(outs):
        first = (half ^ 1 ^ n) * shift
        for q in range(slots):
            for h in range(splits):
                start = part_start(h, part) if splits > 1 else 0
                pairs.append(
                    (
                        down.at[picks[first + q], :, pl.ds(start, part)],
                        out.at[pl.ds(q * rank, rank), pl.ds(h * part, part)],
                    )
                )
    for copy in run_copies(pairs, sems):
        copy.wait()


def table(lists, block):
    sizes, adapters, tails = lists
    end = jnp.int32(0)
    owner, adapter, limit = jnp.int32(0), jnp.int32(0), jnp.int32(BLOCK)
    for q in range(sizes.shape[0]):
        begin = end
        end = end + sizes[q]
        inside = (begin <= block) & (block < end)
        owner = jnp.where(inside, q, owner)
        adapter = jnp.where(inside, adapters[q], adapter)
        limit = jnp.where(inside & (block == end - 1), tails[q], limit)
    return owner, adapter, limit


def token_places(group, rows, chunks):
    near = [(s * rows, rows) for s in range(min(group, 2))]
    far = [(s * rows + row, deep) for s in range(2, group) for row, deep in chunks]
    return near + far


def low_kernel(
    group, layers, rows, chunks, depth, rank, entries, count, by_request, shift, has_sum, last, *refs
):
    lists, refs = refs[:3], refs[3:]
    places = token_places(group, rows, chunks)
    toks, refs = refs[: len(places)], refs[len(places) :]
    arrays, refs = refs[:count], refs[count:]
    if has_sum:
        before, refs = refs[0], refs[1:]
    if last:
        even, odd, refs = refs[0], refs[1], refs[2:]
    else:
        after, refs = refs[0], refs[1:]
    held, refs = refs[0], refs[1:]
    downs, refs = refs[:count], refs[count:]
    tok_sems, sems = refs
    local_blocks = rows // BLOCK
    me = lax.axis_index("batch")
    layer, spot = me // group, me % group
    first = {}
    started = {}
    for n, (t, a, _) in enumerate(entries):
        if a not in started:
            started[a] = pltpu.make_async_copy(arrays[a], downs[a], sems.at[a])
            started[a].start()
        first[t] = []
        for i, (to, deep) in enumerate(places):
            copy = pltpu.make_async_copy(
                toks[i].at[:, pl.ds(t * depth, depth)],
                held.at[pl.ds(to, deep), pl.ds(n * depth, depth)],
                tok_sems.at[i, n],
            )
            copy.start()
            first[t].append(copy)
    slots = []
    for s in range(group):
        for j in range(local_blocks):
            block = (layer * group + (spot ^ s)) * local_blocks + j
            owner, adapter, _ = table(lists, block)
            slots.append(owner - (layer * 2) // layers * shift if by_request else adapter)
    ready = set()
    wide = 2 * local_blocks
    sums = [before[p] if has_sum else None for p in range(group // 2)]
    for n, (t, a, row) in enumerate(entries):
        for copy in first[t]:
            copy.wait()
        if a not in ready:
            started[a].wait()
            ready.add(a)
        for p in range(group // 2):
            chosen = jnp.concatenate(
                [
                    downs[a][pl.ds(pl.multiple_of(row + slots[p * wide + i] * rank, rank), rank), :]
                    for i in range(wide)
                ],
                0,
            )
            term = lax.dot_general(
                held[2 * p * rows : 2 * (p + 1) * rows, n * depth : (n + 1) * depth],
                chosen,
                (((1,), (1,)), ((), ())),
                preferred_element_type=jnp.float32,
            )
            sums[p] = term if sums[p] is None else sums[p] + term
    for p in range(group // 2):
        if not last:
            after[p] = sums[p]
            continue
        for out, at in ((even, 0), (odd, 1)):
            out[p] = jnp.concatenate(
                [
                    sums[p][
                        (at * local_blocks + j) * BLOCK : (at * local_blocks + j + 1) * BLOCK,
                        (at * local_blocks + j) * rank : (at * local_blocks + j + 1) * rank,
                    ]
                    for j in range(local_blocks)
                ],
                1,
            )


def final_kernel(rows, rank, bases, fars, lows, *refs):
    lists, refs = refs[:3], refs[3:]
    far_refs, refs = refs[:fars], refs[fars:]
    base_refs, refs = refs[:bases], refs[bases:]
    low_refs, refs = refs[:lows], refs[lows:]
    ups, out, up_here, sems = refs
    local_blocks = rows // BLOCK
    me = lax.axis_index("batch")
    found = [table(lists, me * local_blocks + j) for j in range(local_blocks)]
    copies = run_copies([(ups.at[found[j][1]], up_here.at[j]) for j in range(local_blocks)], sems)
    low = low_refs[0][...]
    for ref in low_refs[1:]:
        low = low + ref[...]
    low = low.astype(jnp.bfloat16)
    for j in range(local_blocks):
        copies[j].wait()
        here = pl.ds(j * BLOCK, BLOCK)
        total = jnp.dot(
            low[:, j * rank : (j + 1) * rank], up_here[j], preferred_element_type=jnp.float32
        )
        for ref in base_refs:
            total = total + ref[here, :]
        if far_refs:
            total = total + far_refs[0][here, :].astype(jnp.float32)
        live = lax.broadcasted_iota(jnp.int32, total.shape, 0) < found[j][2]
        out[here, :] = jnp.where(live, total, 0.0).astype(jnp.bfloat16)


def shards(
    tokens,
    key_matrix,
    adapter_down_factors,
    adapter_up_factors,
    request_block_list,
    request_adapter_index,
    request_tail_tokens,
):
    rows, width = tokens.shape
    depth, out_width = key_matrix.shape
    adapters, rank = adapter_down_factors.shape[1:]
    reps, devices = lax.axis_size("rep"), lax.axis_size("batch")
    group = 2 * LAYER_CHIPS // reps
    layers = devices // group
    splits = reps if (depth // reps) % LANES == 0 else 1
    part = depth // splits
    local_blocks = rows // BLOCK
    held_width = layers * depth
    lists = (request_block_list, request_adapter_index, request_tail_tokens)
    f32, bf16 = jnp.float32, jnp.bfloat16

    chunks = [
        (sum(PHASES[:i]) * rows // sum(PHASES), PHASES[i] * rows // sum(PHASES))
        for i in range(len(PHASES) if group > 2 else 0)
    ]
    far_count = (group - 2) * len(chunks)
    first = call(
        functools.partial(first_kernel, group, layers, splits, part, chunks),
        [jax.ShapeDtypeStruct((part, out_width), bf16)] * splits
        + [jax.ShapeDtypeStruct((rows, held_width), bf16)] * 2
        + [jax.ShapeDtypeStruct((deep, held_width), bf16) for _, deep in chunks] * (group - 2),
        [HBM] * (splits + 2 + far_count),
        [HBM] * 2,
        [
            pltpu.SemaphoreType.DMA(
                (splits + (2 + far_count) * layers * splits,)
            )
        ],
        0,
        4 * (rows * width + depth * out_width),
    )(key_matrix, tokens)
    key_parts, first = first[:splits], first[splits:]

    far = [list(first[2 + s * len(chunks) :][: len(chunks)]) for s in range(group - 2)]
    sent = []
    for j, (_, deep) in enumerate(chunks):
        if j:
            sent = stack([[(f[j], 0, deep)] for f in far], *[f[j - 1] for f in far], us=WAITS["far"])
        else:
            sent = [f[j] for f in far]
        for s, f in enumerate(far):
            f[j] = swap(sent[s], "batch", 2 + s)

    down = jnp.transpose(adapter_down_factors, (1, 2, 0))
    requests = request_adapter_index.shape[0]
    by_request = requests < adapters
    shift = 1 if by_request and local_blocks * devices == 2 * MOST and layers > 1 else 0
    slots = requests - shift if by_request else adapters
    if by_request:
        across, down = call(
            functools.partial(chosen_kernel, slots, rank, splits, part, group, layers, shift),
            [jax.ShapeDtypeStruct((slots * rank, depth), bf16)] * 2,
            [VMEM] * 2,
            [SMEM, HBM],
            [pltpu.SemaphoreType.DMA((2 * slots * splits,))],
            0,
            8 * slots * rank * depth,
        )(request_adapter_index, down)
    else:
        down = down.reshape(slots * rank, depth)
        across = down

    def over_layers(across, near):
        bundles = []
        bit = layers // 2
        while bit:
            moved = [([bit], swap(near if bundles else across, "batch", bit * group))]
            if bundles:
                rest = [v for _, v in bundles]
                rest = rest[0] if len(rest) == 1 else jnp.concatenate(rest, 0)
                order = [t ^ bit for ts, _ in bundles for t in ts]
                moved.append((order, swap(rest, "batch", bit * group)))
            bundles = bundles + moved
            bit //= 2
        return bundles

    key_bundles = over_layers(key_parts[0], key_parts[0])
    rows_of_key = {}
    for h in range(splits):
        rows_of_key[0, h] = (key_parts[h], 0, part)
    for ts, value in key_bundles:
        for i, t in enumerate(ts):
            rows_of_key[t, 0] = (value, i * part, part)
    last_keys = [key_bundles[-1][1]]
    xcut = CFG.get("xcut", 1)
    for h in range(1, splits):
        swapped = None
        for bundles in (key_bundles[:xcut], key_bundles[xcut:]):
            if not bundles:
                continue
            values = bundles[0][1]
            ready = [swapped] if swapped is not None and (len(bundles) > 1 or CFG.get("x3g")) else []
            if len(bundles) > 1 or ready:
                values = stack([[(v, 0, v.shape[0]) for _, v in bundles]], *ready, us=WAITS["keys"])[0]
            last_keys = [values]
            swapped = swap(values, "rep", h)
            for i, t in enumerate([t for ts, _ in bundles for t in ts]):
                rows_of_key[t, h] = (swapped, i * part, part)
    keys = stack(
        [[rows_of_key[t, h] for t in range(layers) for h in range(splits)]], us=WAITS["all"]
    )[0]

    across_sent = gate(across, *[v for _, v in key_bundles[:CFG.get('z3', 2)]], us=WAITS["across"])
    down_sent = gate(down, *last_keys, us=WAITS["near"])
    if CFG.get("zdirect") and layers == 4:
        d = {2: swap(across_sent, "batch", 2 * group)}
        sent3 = gate(across, *[{"k3": last_keys[0], "Z3": d[2], "gZ5": down_sent}[k] for k in CFG.get("z6", ["k3"])], us=WAITS.get("z6", 0))
        d[1] = swap(down_sent, "batch", group)
        d[3] = swap(sent3, "batch", 3 * group)
        down_bundles = [([t], d[t]) for t in (2, 1, 3)]
    else:
        down_bundles = over_layers(across_sent, down_sent)

    cm = CFG.get("c", 2)
    near = [first[0], swap(gate(first[1], *[v for _, v in down_bundles[:cm]]) if cm else first[1], "batch", 1)]

    def base_of(value):
        return jnp.dot(value, keys, preferred_element_type=f32)

    fars = []
    if far:
        sums = []
        for j in range(len(chunks)):
            theirs = swap(base_of(far[1][j]), "batch", 1)
            sums.append((base_of(far[0][j]) + theirs).astype(bf16))
        if CFG.get("ymerge"):
            sums = [jnp.concatenate(sums, 0)]
        if CFG.get("lowe"):
            down = gate(down, sums[0])
        fars = [swap(v, "batch", 2) for v in sums]
        if CFG.get("lowl"):
            order, value = down_bundles[-1]
            down_bundles[-1] = (order, gate(value, fars[0]))
        fars = [fars[0] if len(fars) == 1 else jnp.concatenate(fars, 0)]
    bases = [base_of(near[0]), swap(base_of(near[1]), "batch", 1)]
    tokens_here = near + [value for f in far for value in f]

    def low_call(bundles, before, last):
        taken = [value for _, value in bundles]
        at = [
            (t, a, i * slots * rank) for a, (ts, _) in enumerate(bundles) for i, t in enumerate(ts)
        ]
        pairs, tall, wide = group // 2, 2 * rows, 2 * local_blocks * rank
        if last:
            outs = [jax.ShapeDtypeStruct((pairs, BLOCK, local_blocks * rank), f32)] * 2
            out_specs = [VMEM] * 2
        else:
            outs, out_specs = jax.ShapeDtypeStruct((pairs, tall, wide), f32), VMEM
        return call(
            functools.partial(
                low_kernel, group, layers, rows, chunks, depth, rank, tuple(at), len(taken), by_request,
                shift, before is not None, last,
            ),
            outs,
            out_specs,
            [SMEM] * 3 + [HBM] * (len(tokens_here) + len(taken)) + [VMEM] * (before is not None),
            [pltpu.VMEM((group * rows, len(at) * depth), bf16)]
            + [pltpu.VMEM(v.shape, bf16) for v in taken]
            + [pltpu.SemaphoreType.DMA((len(tokens_here), len(at))), pltpu.SemaphoreType.DMA((len(taken),))],
            WAITS["low"][last] * CORE_FLOPS_PER_US,
            0,
        )(*lists, *tokens_here, *taken, *([before] if before is not None else []))

    early = low_call([([0], down)] + down_bundles[:-1], None, False)
    even, odd = low_call(down_bundles[-1:], early, True)
    got = swap(odd, "batch", 1)
    lows = layer_pairs(even, got)

    return call(
        functools.partial(final_kernel, rows, rank, len(bases), len(fars), len(lows)),
        jax.ShapeDtypeStruct((rows, out_width), bf16),
        VMEM,
        [SMEM] * 3 + [VMEM] * (len(fars) + len(bases) + len(lows)) + [HBM],
        [pltpu.VMEM((local_blocks, rank, out_width), bf16), pltpu.SemaphoreType.DMA((local_blocks,))],
        2 * rows * rank * out_width,
        8 * rows * out_width,
    )(*lists, *fars, *bases, *lows, adapter_up_factors)


def layer_pairs(mine, got):
    bit = 2
    while mine.shape[0] > 1:
        total = mine + got
        mine, got = total[0::2], swap(total[1::2], "batch", bit)
        bit *= 2
    return [mine[0], got[0]]


def solution(mesh):
    placed = (
        P(("rep", "batch"), None),
        P("batch", None),
        P("batch", None, None),
        P(),
        P("rep"),
        P("rep"),
        P("rep"),
    )
    return jax.shard_map(
        shards, mesh=mesh, in_specs=placed, out_specs=P(("rep", "batch"), None), check_vma=False
    )
```

```python
import functools

import jax
import jax.numpy as jnp
from jax import lax
from jax.experimental import pallas as pl
from jax.experimental.pallas import tpu as pltpu
from jax.sharding import PartitionSpec as P

BLOCK = 128
LANES = 128
MOST = 16
LAYER_CHIPS = 4
VMEM_BYTES = 28 * 1024 * 1024
CORE_FLOPS_PER_US = 1_153_500_000
CFG = {'us': {'all': 30, 'far': 2}, 'z3': 2, 'c': 'W', 'xcut': 2, 'ph': [11, 5]}
WAITS = {"far": 12, "keys": 0, "all": 5, "across": 0, "near": 0, "low": (5, 15)}
WAITS.update(CFG.get("us", {}))
PHASES = tuple(CFG.get("ph", [8, 8]))

HBM = pl.BlockSpec(memory_space=pl.ANY)
VMEM = pl.BlockSpec(memory_space=pltpu.VMEM)
SMEM = pl.BlockSpec(memory_space=pltpu.SMEM)


def call(kernel, outs, out_specs, in_specs, scratch, flops, moved):
    return pl.pallas_call(
        kernel,
        out_shape=outs,
        in_specs=in_specs,
        out_specs=out_specs,
        scratch_shapes=scratch,
        compiler_params=pltpu.CompilerParams(vmem_limit_bytes=VMEM_BYTES),
        cost_estimate=pl.CostEstimate(flops=flops, bytes_accessed=moved, transcendentals=0),
    )


def swap(value, axis, bit):
    return lax.ppermute(value, axis, [(i, i ^ bit) for i in range(lax.axis_size(axis))])


def run_copies(pairs, sems):
    copies = [pltpu.make_async_copy(a, b, sems.at[i]) for i, (a, b) in enumerate(pairs)]
    for copy in copies:
        copy.start()
    return copies


def part_start(h, part):
    return pl.multiple_of((lax.axis_index("rep") ^ h) * part, part)


def first_kernel(group, layers, splits, part, chunks, key, tokens, *refs):
    keys, refs = refs[:splits], refs[splits:]
    outs, sems = refs[:-1], refs[-1]
    depth = splits * part
    me = lax.axis_index("batch")
    layer, spot = me // group, me % group
    pairs = [(key.at[pl.ds(part_start(h, part), part), :], keys[h]) for h in range(splits)]
    for s in reversed(range(group)):
        for t in range(layers):
            first = ((layer ^ t) * group + (spot ^ s)) * depth
            for h in range(splits):
                start = first + part_start(h, part) if splits > 1 else first
                start = pl.multiple_of(start, part)
                to = pl.ds(t * depth + h * part, part)
                if s < 2:
                    pairs.append((tokens.at[:, pl.ds(start, part)], outs[s].at[:, to]))
                    continue
                for j, (row, deep) in enumerate(chunks):
                    pairs.append(
                        (
                            tokens.at[pl.ds(row, deep), pl.ds(start, part)],
                            outs[2 + (s - 2) * len(chunks) + j].at[:, to],
                        )
                    )
    for copy in run_copies(pairs, sems):
        copy.wait()


def stack_kernel(moves, taken, count, *refs):
    values, outs, sems = refs[:taken], refs[count:-1], refs[-1]
    pairs = []
    for o, to, a, row, rows in moves:
        pairs.append((values[a].at[pl.ds(row, rows), :], outs[o].at[pl.ds(to, rows), :]))
    for copy in run_copies(pairs, sems):
        copy.wait()


def stack(lists, *ready, us=0):
    values, moves, outs = [], [], []
    for o, rows_of in enumerate(lists):
        to = 0
        for value, row, rows in rows_of:
            moves.append((o, to, len(values), row, rows))
            values.append(value)
            to += rows
        outs.append(jax.ShapeDtypeStruct((to, value.shape[1]), value.dtype))
    count = len(values) + len(ready)
    return call(
        functools.partial(stack_kernel, tuple(moves), len(values), count),
        outs,
        [VMEM] * len(outs),
        [HBM] * count,
        [pltpu.SemaphoreType.DMA((len(moves),))],
        us * CORE_FLOPS_PER_US,
        0,
    )(*values, *ready)


def gate(value, *ready, us=0):
    return stack([[(value, 0, value.shape[0])]], *ready, us=us)[0]


def chosen_kernel(slots, rank, splits, part, group, layers, shift, picks, down, *refs):
    outs, sems = refs[:-1], refs[-1]
    layer = lax.axis_index("batch") // group
    half = (layer * 2) // layers
    pairs = []
    for n, out in enumerate(outs):
        first = (half ^ 1 ^ n) * shift
        for q in range(slots):
            for h in range(splits):
                start = part_start(h, part) if splits > 1 else 0
                pairs.append(
                    (
                        down.at[picks[first + q], :, pl.ds(start, part)],
                        out.at[pl.ds(q * rank, rank), pl.ds(h * part, part)],
                    )
                )
    for copy in run_copies(pairs, sems):
        copy.wait()


def table(lists, block):
    sizes, adapters, tails = lists
    end = jnp.int32(0)
    owner, adapter, limit = jnp.int32(0), jnp.int32(0), jnp.int32(BLOCK)
    for q in range(sizes.shape[0]):
        begin = end
        end = end + sizes[q]
        inside = (begin <= block) & (block < end)
        owner = jnp.where(inside, q, owner)
        adapter = jnp.where(inside, adapters[q], adapter)
        limit = jnp.where(inside & (block == end - 1), tails[q], limit)
    return owner, adapter, limit


def token_places(group, rows, chunks):
    near = [(s * rows, rows) for s in range(min(group, 2))]
    far = [(s * rows + row, deep) for s in range(2, group) for row, deep in chunks]
    return near + far


def low_kernel(
    group, layers, rows, chunks, depth, rank, entries, count, by_request, shift, has_sum, last, *refs
):
    lists, refs = refs[:3], refs[3:]
    places = token_places(group, rows, chunks)
    toks, refs = refs[: len(places)], refs[len(places) :]
    arrays, refs = refs[:count], refs[count:]
    if has_sum:
        before, refs = refs[0], refs[1:]
    if last:
        even, odd, refs = refs[0], refs[1], refs[2:]
    else:
        after, refs = refs[0], refs[1:]
    held, refs = refs[0], refs[1:]
    downs, refs = refs[:count], refs[count:]
    tok_sems, sems = refs
    local_blocks = rows // BLOCK
    me = lax.axis_index("batch")
    layer, spot = me // group, me % group
    first = {}
    started = {}
    for n, (t, a, _) in enumerate(entries):
        if a not in started:
            started[a] = pltpu.make_async_copy(arrays[a], downs[a], sems.at[a])
            started[a].start()
        first[t] = []
        for i, (to, deep) in enumerate(places):
            copy = pltpu.make_async_copy(
                toks[i].at[:, pl.ds(t * depth, depth)],
                held.at[pl.ds(to, deep), pl.ds(n * depth, depth)],
                tok_sems.at[i, n],
            )
            copy.start()
            first[t].append(copy)
    slots = []
    for s in range(group):
        for j in range(local_blocks):
            block = (layer * group + (spot ^ s)) * local_blocks + j
            owner, adapter, _ = table(lists, block)
            slots.append(owner - (layer * 2) // layers * shift if by_request else adapter)
    ready = set()
    wide = 2 * local_blocks
    sums = [before[p] if has_sum else None for p in range(group // 2)]
    for n, (t, a, row) in enumerate(entries):
        for copy in first[t]:
            copy.wait()
        if a not in ready:
            started[a].wait()
            ready.add(a)
        for p in range(group // 2):
            chosen = jnp.concatenate(
                [
                    downs[a][pl.ds(pl.multiple_of(row + slots[p * wide + i] * rank, rank), rank), :]
                    for i in range(wide)
                ],
                0,
            )
            term = lax.dot_general(
                held[2 * p * rows : 2 * (p + 1) * rows, n * depth : (n + 1) * depth],
                chosen,
                (((1,), (1,)), ((), ())),
                preferred_element_type=jnp.float32,
            )
            sums[p] = term if sums[p] is None else sums[p] + term
    for p in range(group // 2):
        if not last:
            after[p] = sums[p]
            continue
        for out, at in ((even, 0), (odd, 1)):
            out[p] = jnp.concatenate(
                [
                    sums[p][
                        (at * local_blocks + j) * BLOCK : (at * local_blocks + j + 1) * BLOCK,
                        (at * local_blocks + j) * rank : (at * local_blocks + j + 1) * rank,
                    ]
                    for j in range(local_blocks)
                ],
                1,
            )


def final_kernel(rows, rank, bases, fars, lows, *refs):
    lists, refs = refs[:3], refs[3:]
    far_refs, refs = refs[:fars], refs[fars:]
    base_refs, refs = refs[:bases], refs[bases:]
    low_refs, refs = refs[:lows], refs[lows:]
    ups, out, up_here, sems = refs
    local_blocks = rows // BLOCK
    me = lax.axis_index("batch")
    found = [table(lists, me * local_blocks + j) for j in range(local_blocks)]
    copies = run_copies([(ups.at[found[j][1]], up_here.at[j]) for j in range(local_blocks)], sems)
    low = low_refs[0][...]
    for ref in low_refs[1:]:
        low = low + ref[...]
    low = low.astype(jnp.bfloat16)
    for j in range(local_blocks):
        copies[j].wait()
        here = pl.ds(j * BLOCK, BLOCK)
        total = jnp.dot(
            low[:, j * rank : (j + 1) * rank], up_here[j], preferred_element_type=jnp.float32
        )
        for ref in base_refs:
            total = total + ref[here, :]
        if far_refs:
            total = total + far_refs[0][here, :].astype(jnp.float32)
        live = lax.broadcasted_iota(jnp.int32, total.shape, 0) < found[j][2]
        out[here, :] = jnp.where(live, total, 0.0).astype(jnp.bfloat16)


def shards(
    tokens,
    key_matrix,
    adapter_down_factors,
    adapter_up_factors,
    request_block_list,
    request_adapter_index,
    request_tail_tokens,
):
    rows, width = tokens.shape
    depth, out_width = key_matrix.shape
    adapters, rank = adapter_down_factors.shape[1:]
    reps, devices = lax.axis_size("rep"), lax.axis_size("batch")
    group = 2 * LAYER_CHIPS // reps
    layers = devices // group
    splits = reps if (depth // reps) % LANES == 0 else 1
    part = depth // splits
    local_blocks = rows // BLOCK
    held_width = layers * depth
    lists = (request_block_list, request_adapter_index, request_tail_tokens)
    f32, bf16 = jnp.float32, jnp.bfloat16

    chunks = [
        (sum(PHASES[:i]) * rows // sum(PHASES), PHASES[i] * rows // sum(PHASES))
        for i in range(len(PHASES) if group > 2 else 0)
    ]
    far_count = (group - 2) * len(chunks)
    first = call(
        functools.partial(first_kernel, group, layers, splits, part, chunks),
        [jax.ShapeDtypeStruct((part, out_width), bf16)] * splits
        + [jax.ShapeDtypeStruct((rows, held_width), bf16)] * 2
        + [jax.ShapeDtypeStruct((deep, held_width), bf16) for _, deep in chunks] * (group - 2),
        [HBM] * (splits + 2 + far_count),
        [HBM] * 2,
        [
            pltpu.SemaphoreType.DMA(
                (splits + (2 + far_count) * layers * splits,)
            )
        ],
        0,
        4 * (rows * width + depth * out_width),
    )(key_matrix, tokens)
    key_parts, first = first[:splits], first[splits:]

    far = [list(first[2 + s * len(chunks) :][: len(chunks)]) for s in range(group - 2)]
    sent = []
    for j, (_, deep) in enumerate(chunks):
        if j:
            sent = stack([[(f[j], 0, deep)] for f in far], *[f[j - 1] for f in far], us=WAITS["far"])
        else:
            sent = [f[j] for f in far]
        for s, f in enumerate(far):
            f[j] = swap(sent[s], "batch", 2 + s)

    down = jnp.transpose(adapter_down_factors, (1, 2, 0))
    requests = request_adapter_index.shape[0]
    by_request = requests < adapters
    shift = 1 if by_request and local_blocks * devices == 2 * MOST and layers > 1 else 0
    slots = requests - shift if by_request else adapters
    if by_request:
        across, down = call(
            functools.partial(chosen_kernel, slots, rank, splits, part, group, layers, shift),
            [jax.ShapeDtypeStruct((slots * rank, depth), bf16)] * 2,
            [VMEM] * 2,
            [SMEM, HBM],
            [pltpu.SemaphoreType.DMA((2 * slots * splits,))],
            0,
            8 * slots * rank * depth,
        )(request_adapter_index, down)
    else:
        down = down.reshape(slots * rank, depth)
        across = down

    def over_layers(across, near):
        bundles = []
        bit = layers // 2
        while bit:
            moved = [([bit], swap(near if bundles else across, "batch", bit * group))]
            if bundles:
                rest = [v for _, v in bundles]
                rest = rest[0] if len(rest) == 1 else jnp.concatenate(rest, 0)
                order = [t ^ bit for ts, _ in bundles for t in ts]
                moved.append((order, swap(rest, "batch", bit * group)))
            bundles = bundles + moved
            bit //= 2
        return bundles

    key_bundles = over_layers(key_parts[0], key_parts[0])
    rows_of_key = {}
    for h in range(splits):
        rows_of_key[0, h] = (key_parts[h], 0, part)
    for ts, value in key_bundles:
        for i, t in enumerate(ts):
            rows_of_key[t, 0] = (value, i * part, part)
    last_keys = [key_bundles[-1][1]]
    xcut = CFG.get("xcut", 1)
    for h in range(1, splits):
        swapped = None
        for bundles in (key_bundles[:xcut], key_bundles[xcut:]):
            if not bundles:
                continue
            values = bundles[0][1]
            ready = [swapped] if swapped is not None and (len(bundles) > 1 or CFG.get("x3g")) else []
            if len(bundles) > 1 or ready:
                values = stack([[(v, 0, v.shape[0]) for _, v in bundles]], *ready, us=WAITS["keys"])[0]
            last_keys = [values]
            swapped = swap(values, "rep", h)
            for i, t in enumerate([t for ts, _ in bundles for t in ts]):
                rows_of_key[t, h] = (swapped, i * part, part)
    keys = stack(
        [[rows_of_key[t, h] for t in range(layers) for h in range(splits)]], us=WAITS["all"]
    )[0]

    across_sent = gate(across, *[v for _, v in key_bundles[:CFG.get('z3', 2)]], us=WAITS["across"])
    down_sent = gate(down, *last_keys, us=WAITS["near"])
    if CFG.get("zdirect") and layers == 4:
        d = {2: swap(across_sent, "batch", 2 * group)}
        sent3 = gate(across, *[{"k3": last_keys[0], "Z3": d[2], "gZ5": down_sent}[k] for k in CFG.get("z6", ["k3"])], us=WAITS.get("z6", 0))
        d[1] = swap(down_sent, "batch", group)
        d[3] = swap(sent3, "batch", 3 * group)
        down_bundles = [([t], d[t]) for t in (2, 1, 3)]
    else:
        down_bundles = over_layers(across_sent, down_sent)

    cm = CFG.get("c", 2)
    c_ready = {"W": [keys], "Z3W": [keys, down_bundles[0][1]], "X": [swapped] if splits > 1 else []}.get(cm) if isinstance(cm, str) else [v for _, v in down_bundles[:cm]]
    near = [first[0], swap(gate(first[1], *c_ready) if cm else first[1], "batch", 1)]

    def base_of(value):
        return jnp.dot(value, keys, preferred_element_type=f32)

    fars = []
    if far:
        sums = []
        for j in range(len(chunks)):
            theirs = swap(base_of(far[1][j]), "batch", 1)
            sums.append((base_of(far[0][j]) + theirs).astype(bf16))
        if CFG.get("ymerge"):
            sums = [jnp.concatenate(sums, 0)]
        if CFG.get("lowe"):
            down = gate(down, sums[0])
        fars = [swap(v, "batch", 2) for v in sums]
        if CFG.get("lowl"):
            order, value = down_bundles[-1]
            down_bundles[-1] = (order, gate(value, fars[0]))
        fars = [fars[0] if len(fars) == 1 else jnp.concatenate(fars, 0)]
    bases = [base_of(near[0]), swap(base_of(near[1]), "batch", 1)]
    tokens_here = near + [value for f in far for value in f]

    def low_call(bundles, before, last):
        taken = [value for _, value in bundles]
        at = [
            (t, a, i * slots * rank) for a, (ts, _) in enumerate(bundles) for i, t in enumerate(ts)
        ]
        pairs, tall, wide = group // 2, 2 * rows, 2 * local_blocks * rank
        if last:
            outs = [jax.ShapeDtypeStruct((pairs, BLOCK, local_blocks * rank), f32)] * 2
            out_specs = [VMEM] * 2
        else:
            outs, out_specs = jax.ShapeDtypeStruct((pairs, tall, wide), f32), VMEM
        return call(
            functools.partial(
                low_kernel, group, layers, rows, chunks, depth, rank, tuple(at), len(taken), by_request,
                shift, before is not None, last,
            ),
            outs,
            out_specs,
            [SMEM] * 3 + [HBM] * (len(tokens_here) + len(taken)) + [VMEM] * (before is not None),
            [pltpu.VMEM((group * rows, len(at) * depth), bf16)]
            + [pltpu.VMEM(v.shape, bf16) for v in taken]
            + [pltpu.SemaphoreType.DMA((len(tokens_here), len(at))), pltpu.SemaphoreType.DMA((len(taken),))],
            WAITS["low"][last] * CORE_FLOPS_PER_US,
            0,
        )(*lists, *tokens_here, *taken, *([before] if before is not None else []))

    early = low_call([([0], down)] + down_bundles[:-1], None, False)
    even, odd = low_call(down_bundles[-1:], early, True)
    got = swap(odd, "batch", 1)
    lows = layer_pairs(even, got)

    return call(
        functools.partial(final_kernel, rows, rank, len(bases), len(fars), len(lows)),
        jax.ShapeDtypeStruct((rows, out_width), bf16),
        VMEM,
        [SMEM] * 3 + [VMEM] * (len(fars) + len(bases) + len(lows)) + [HBM],
        [pltpu.VMEM((local_blocks, rank, out_width), bf16), pltpu.SemaphoreType.DMA((local_blocks,))],
        2 * rows * rank * out_width,
        8 * rows * out_width,
    )(*lists, *fars, *bases, *lows, adapter_up_factors)


def layer_pairs(mine, got):
    bit = 2
    while mine.shape[0] > 1:
        total = mine + got
        mine, got = total[0::2], swap(total[1::2], "batch", bit)
        bit *= 2
    return [mine[0], got[0]]


def solution(mesh):
    placed = (
        P(("rep", "batch"), None),
        P("batch", None),
        P("batch", None, None),
        P(),
        P("rep"),
        P("rep"),
        P("rep"),
    )
    return jax.shard_map(
        shards, mesh=mesh, in_specs=placed, out_specs=P(("rep", "batch"), None), check_vma=False
    )
```

```python
import functools

import jax
import jax.numpy as jnp
from jax import lax
from jax.experimental import pallas as pl
from jax.experimental.pallas import tpu as pltpu
from jax.sharding import PartitionSpec as P

BLOCK = 128
LANES = 128
MOST = 16
LAYER_CHIPS = 4
VMEM_BYTES = 28 * 1024 * 1024
CORE_FLOPS_PER_US = 1_153_500_000
CFG = {'us': {'all': 30, 'far': 12}, 'z3': 2, 'c': 'W', 'xcut': 2, 'ph': [13, 3]}
WAITS = {"far": 12, "keys": 0, "all": 5, "across": 0, "near": 0, "low": (5, 15)}
WAITS.update(CFG.get("us", {}))
PHASES = tuple(CFG.get("ph", [8, 8]))

HBM = pl.BlockSpec(memory_space=pl.ANY)
VMEM = pl.BlockSpec(memory_space=pltpu.VMEM)
SMEM = pl.BlockSpec(memory_space=pltpu.SMEM)


def call(kernel, outs, out_specs, in_specs, scratch, flops, moved):
    return pl.pallas_call(
        kernel,
        out_shape=outs,
        in_specs=in_specs,
        out_specs=out_specs,
        scratch_shapes=scratch,
        compiler_params=pltpu.CompilerParams(vmem_limit_bytes=VMEM_BYTES),
        cost_estimate=pl.CostEstimate(flops=flops, bytes_accessed=moved, transcendentals=0),
    )


def swap(value, axis, bit):
    return lax.ppermute(value, axis, [(i, i ^ bit) for i in range(lax.axis_size(axis))])


def run_copies(pairs, sems):
    copies = [pltpu.make_async_copy(a, b, sems.at[i]) for i, (a, b) in enumerate(pairs)]
    for copy in copies:
        copy.start()
    return copies


def part_start(h, part):
    return pl.multiple_of((lax.axis_index("rep") ^ h) * part, part)


def first_kernel(group, layers, splits, part, chunks, key, tokens, *refs):
    keys, refs = refs[:splits], refs[splits:]
    outs, sems = refs[:-1], refs[-1]
    depth = splits * part
    me = lax.axis_index("batch")
    layer, spot = me // group, me % group
    pairs = [(key.at[pl.ds(part_start(h, part), part), :], keys[h]) for h in range(splits)]
    for s in reversed(range(group)):
        for t in range(layers):
            first = ((layer ^ t) * group + (spot ^ s)) * depth
            for h in range(splits):
                start = first + part_start(h, part) if splits > 1 else first
                start = pl.multiple_of(start, part)
                to = pl.ds(t * depth + h * part, part)
                if s < 2:
                    pairs.append((tokens.at[:, pl.ds(start, part)], outs[s].at[:, to]))
                    continue
                for j, (row, deep) in enumerate(chunks):
                    pairs.append(
                        (
                            tokens.at[pl.ds(row, deep), pl.ds(start, part)],
                            outs[2 + (s - 2) * len(chunks) + j].at[:, to],
                        )
                    )
    for copy in run_copies(pairs, sems):
        copy.wait()


def stack_kernel(moves, taken, count, *refs):
    values, outs, sems = refs[:taken], refs[count:-1], refs[-1]
    pairs = []
    for o, to, a, row, rows in moves:
        pairs.append((values[a].at[pl.ds(row, rows), :], outs[o].at[pl.ds(to, rows), :]))
    for copy in run_copies(pairs, sems):
        copy.wait()


def stack(lists, *ready, us=0):
    values, moves, outs = [], [], []
    for o, rows_of in enumerate(lists):
        to = 0
        for value, row, rows in rows_of:
            moves.append((o, to, len(values), row, rows))
            values.append(value)
            to += rows
        outs.append(jax.ShapeDtypeStruct((to, value.shape[1]), value.dtype))
    count = len(values) + len(ready)
    return call(
        functools.partial(stack_kernel, tuple(moves), len(values), count),
        outs,
        [VMEM] * len(outs),
        [HBM] * count,
        [pltpu.SemaphoreType.DMA((len(moves),))],
        us * CORE_FLOPS_PER_US,
        0,
    )(*values, *ready)


def gate(value, *ready, us=0):
    return stack([[(value, 0, value.shape[0])]], *ready, us=us)[0]


def chosen_kernel(slots, rank, splits, part, group, layers, shift, picks, down, *refs):
    outs, sems = refs[:-1], refs[-1]
    layer = lax.axis_index("batch") // group
    half = (layer * 2) // layers
    pairs = []
    for n, out in enumerate(outs):
        first = (half ^ 1 ^ n) * shift
        for q in range(slots):
            for h in range(splits):
                start = part_start(h, part) if splits > 1 else 0
                pairs.append(
                    (
                        down.at[picks[first + q], :, pl.ds(start, part)],
                        out.at[pl.ds(q * rank, rank), pl.ds(h * part, part)],
                    )
                )
    for copy in run_copies(pairs, sems):
        copy.wait()


def table(lists, block):
    sizes, adapters, tails = lists
    end = jnp.int32(0)
    owner, adapter, limit = jnp.int32(0), jnp.int32(0), jnp.int32(BLOCK)
    for q in range(sizes.shape[0]):
        begin = end
        end = end + sizes[q]
        inside = (begin <= block) & (block < end)
        owner = jnp.where(inside, q, owner)
        adapter = jnp.where(inside, adapters[q], adapter)
        limit = jnp.where(inside & (block == end - 1), tails[q], limit)
    return owner, adapter, limit


def token_places(group, rows, chunks):
    near = [(s * rows, rows) for s in range(min(group, 2))]
    far = [(s * rows + row, deep) for s in range(2, group) for row, deep in chunks]
    return near + far


def low_kernel(
    group, layers, rows, chunks, depth, rank, entries, count, by_request, shift, has_sum, last, *refs
):
    lists, refs = refs[:3], refs[3:]
    places = token_places(group, rows, chunks)
    toks, refs = refs[: len(places)], refs[len(places) :]
    arrays, refs = refs[:count], refs[count:]
    if has_sum:
        before, refs = refs[0], refs[1:]
    if last:
        even, odd, refs = refs[0], refs[1], refs[2:]
    else:
        after, refs = refs[0], refs[1:]
    held, refs = refs[0], refs[1:]
    downs, refs = refs[:count], refs[count:]
    tok_sems, sems = refs
    local_blocks = rows // BLOCK
    me = lax.axis_index("batch")
    layer, spot = me // group, me % group
    first = {}
    started = {}
    for n, (t, a, _) in enumerate(entries):
        if a not in started:
            started[a] = pltpu.make_async_copy(arrays[a], downs[a], sems.at[a])
            started[a].start()
        first[t] = []
        for i, (to, deep) in enumerate(places):
            copy = pltpu.make_async_copy(
                toks[i].at[:, pl.ds(t * depth, depth)],
                held.at[pl.ds(to, deep), pl.ds(n * depth, depth)],
                tok_sems.at[i, n],
            )
            copy.start()
            first[t].append(copy)
    slots = []
    for s in range(group):
        for j in range(local_blocks):
            block = (layer * group + (spot ^ s)) * local_blocks + j
            owner, adapter, _ = table(lists, block)
            slots.append(owner - (layer * 2) // layers * shift if by_request else adapter)
    ready = set()
    wide = 2 * local_blocks
    sums = [before[p] if has_sum else None for p in range(group // 2)]
    for n, (t, a, row) in enumerate(entries):
        for copy in first[t]:
            copy.wait()
        if a not in ready:
            started[a].wait()
            ready.add(a)
        for p in range(group // 2):
            chosen = jnp.concatenate(
                [
                    downs[a][pl.ds(pl.multiple_of(row + slots[p * wide + i] * rank, rank), rank), :]
                    for i in range(wide)
                ],
                0,
            )
            term = lax.dot_general(
                held[2 * p * rows : 2 * (p + 1) * rows, n * depth : (n + 1) * depth],
                chosen,
                (((1,), (1,)), ((), ())),
                preferred_element_type=jnp.float32,
            )
            sums[p] = term if sums[p] is None else sums[p] + term
    for p in range(group // 2):
        if not last:
            after[p] = sums[p]
            continue
        for out, at in ((even, 0), (odd, 1)):
            out[p] = jnp.concatenate(
                [
                    sums[p][
                        (at * local_blocks + j) * BLOCK : (at * local_blocks + j + 1) * BLOCK,
                        (at * local_blocks + j) * rank : (at * local_blocks + j + 1) * rank,
                    ]
                    for j in range(local_blocks)
                ],
                1,
            )


def final_kernel(rows, rank, bases, fars, lows, *refs):
    lists, refs = refs[:3], refs[3:]
    far_refs, refs = refs[:fars], refs[fars:]
    base_refs, refs = refs[:bases], refs[bases:]
    low_refs, refs = refs[:lows], refs[lows:]
    ups, out, up_here, sems = refs
    local_blocks = rows // BLOCK
    me = lax.axis_index("batch")
    found = [table(lists, me * local_blocks + j) for j in range(local_blocks)]
    copies = run_copies([(ups.at[found[j][1]], up_here.at[j]) for j in range(local_blocks)], sems)
    low = low_refs[0][...]
    for ref in low_refs[1:]:
        low = low + ref[...]
    low = low.astype(jnp.bfloat16)
    for j in range(local_blocks):
        copies[j].wait()
        here = pl.ds(j * BLOCK, BLOCK)
        total = jnp.dot(
            low[:, j * rank : (j + 1) * rank], up_here[j], preferred_element_type=jnp.float32
        )
        for ref in base_refs:
            total = total + ref[here, :]
        if far_refs:
            total = total + far_refs[0][here, :].astype(jnp.float32)
        live = lax.broadcasted_iota(jnp.int32, total.shape, 0) < found[j][2]
        out[here, :] = jnp.where(live, total, 0.0).astype(jnp.bfloat16)


def shards(
    tokens,
    key_matrix,
    adapter_down_factors,
    adapter_up_factors,
    request_block_list,
    request_adapter_index,
    request_tail_tokens,
):
    rows, width = tokens.shape
    depth, out_width = key_matrix.shape
    adapters, rank = adapter_down_factors.shape[1:]
    reps, devices = lax.axis_size("rep"), lax.axis_size("batch")
    group = 2 * LAYER_CHIPS // reps
    layers = devices // group
    splits = reps if (depth // reps) % LANES == 0 else 1
    part = depth // splits
    local_blocks = rows // BLOCK
    held_width = layers * depth
    lists = (request_block_list, request_adapter_index, request_tail_tokens)
    f32, bf16 = jnp.float32, jnp.bfloat16

    chunks = [
        (sum(PHASES[:i]) * rows // sum(PHASES), PHASES[i] * rows // sum(PHASES))
        for i in range(len(PHASES) if group > 2 else 0)
    ]
    far_count = (group - 2) * len(chunks)
    first = call(
        functools.partial(first_kernel, group, layers, splits, part, chunks),
        [jax.ShapeDtypeStruct((part, out_width), bf16)] * splits
        + [jax.ShapeDtypeStruct((rows, held_width), bf16)] * 2
        + [jax.ShapeDtypeStruct((deep, held_width), bf16) for _, deep in chunks] * (group - 2),
        [HBM] * (splits + 2 + far_count),
        [HBM] * 2,
        [
            pltpu.SemaphoreType.DMA(
                (splits + (2 + far_count) * layers * splits,)
            )
        ],
        0,
        4 * (rows * width + depth * out_width),
    )(key_matrix, tokens)
    key_parts, first = first[:splits], first[splits:]

    far = [list(first[2 + s * len(chunks) :][: len(chunks)]) for s in range(group - 2)]
    sent = []
    for j, (_, deep) in enumerate(chunks):
        if j:
            sent = stack([[(f[j], 0, deep)] for f in far], *[f[j - 1] for f in far], us=WAITS["far"])
        else:
            sent = [f[j] for f in far]
        for s, f in enumerate(far):
            f[j] = swap(sent[s], "batch", 2 + s)

    down = jnp.transpose(adapter_down_factors, (1, 2, 0))
    requests = request_adapter_index.shape[0]
    by_request = requests < adapters
    shift = 1 if by_request and local_blocks * devices == 2 * MOST and layers > 1 else 0
    slots = requests - shift if by_request else adapters
    if by_request:
        across, down = call(
            functools.partial(chosen_kernel, slots, rank, splits, part, group, layers, shift),
            [jax.ShapeDtypeStruct((slots * rank, depth), bf16)] * 2,
            [VMEM] * 2,
            [SMEM, HBM],
            [pltpu.SemaphoreType.DMA((2 * slots * splits,))],
            0,
            8 * slots * rank * depth,
        )(request_adapter_index, down)
    else:
        down = down.reshape(slots * rank, depth)
        across = down

    def over_layers(across, near):
        bundles = []
        bit = layers // 2
        while bit:
            moved = [([bit], swap(near if bundles else across, "batch", bit * group))]
            if bundles:
                rest = [v for _, v in bundles]
                rest = rest[0] if len(rest) == 1 else jnp.concatenate(rest, 0)
                order = [t ^ bit for ts, _ in bundles for t in ts]
                moved.append((order, swap(rest, "batch", bit * group)))
            bundles = bundles + moved
            bit //= 2
        return bundles

    key_bundles = over_layers(key_parts[0], key_parts[0])
    rows_of_key = {}
    for h in range(splits):
        rows_of_key[0, h] = (key_parts[h], 0, part)
    for ts, value in key_bundles:
        for i, t in enumerate(ts):
            rows_of_key[t, 0] = (value, i * part, part)
    last_keys = [key_bundles[-1][1]]
    xcut = CFG.get("xcut", 1)
    for h in range(1, splits):
        swapped = None
        for bundles in (key_bundles[:xcut], key_bundles[xcut:]):
            if not bundles:
                continue
            values = bundles[0][1]
            ready = [swapped] if swapped is not None and (len(bundles) > 1 or CFG.get("x3g")) else []
            if len(bundles) > 1 or ready:
                values = stack([[(v, 0, v.shape[0]) for _, v in bundles]], *ready, us=WAITS["keys"])[0]
            last_keys = [values]
            swapped = swap(values, "rep", h)
            for i, t in enumerate([t for ts, _ in bundles for t in ts]):
                rows_of_key[t, h] = (swapped, i * part, part)
    keys = stack(
        [[rows_of_key[t, h] for t in range(layers) for h in range(splits)]], us=WAITS["all"]
    )[0]

    across_sent = gate(across, *[v for _, v in key_bundles[:CFG.get('z3', 2)]], us=WAITS["across"])
    down_sent = gate(down, *last_keys, us=WAITS["near"])
    if CFG.get("zdirect") and layers == 4:
        d = {2: swap(across_sent, "batch", 2 * group)}
        sent3 = gate(across, *[{"k3": last_keys[0], "Z3": d[2], "gZ5": down_sent}[k] for k in CFG.get("z6", ["k3"])], us=WAITS.get("z6", 0))
        d[1] = swap(down_sent, "batch", group)
        d[3] = swap(sent3, "batch", 3 * group)
        down_bundles = [([t], d[t]) for t in (2, 1, 3)]
    else:
        down_bundles = over_layers(across_sent, down_sent)

    cm = CFG.get("c", 2)
    c_ready = {"W": [keys], "Z3W": [keys, down_bundles[0][1]], "X": [swapped] if splits > 1 else []}.get(cm) if isinstance(cm, str) else [v for _, v in down_bundles[:cm]]
    near = [first[0], swap(gate(first[1], *c_ready) if cm else first[1], "batch", 1)]

    def base_of(value):
        return jnp.dot(value, keys, preferred_element_type=f32)

    fars = []
    if far:
        sums = []
        for j in range(len(chunks)):
            theirs = swap(base_of(far[1][j]), "batch", 1)
            sums.append((base_of(far[0][j]) + theirs).astype(bf16))
        if CFG.get("ymerge"):
            sums = [jnp.concatenate(sums, 0)]
        if CFG.get("lowe"):
            down = gate(down, sums[0])
        fars = [swap(v, "batch", 2) for v in sums]
        if CFG.get("lowl"):
            order, value = down_bundles[-1]
            down_bundles[-1] = (order, gate(value, fars[0]))
        fars = [fars[0] if len(fars) == 1 else jnp.concatenate(fars, 0)]
    bases = [base_of(near[0]), swap(base_of(near[1]), "batch", 1)]
    tokens_here = near + [value for f in far for value in f]

    def low_call(bundles, before, last):
        taken = [value for _, value in bundles]
        at = [
            (t, a, i * slots * rank) for a, (ts, _) in enumerate(bundles) for i, t in enumerate(ts)
        ]
        pairs, tall, wide = group // 2, 2 * rows, 2 * local_blocks * rank
        if last:
            outs = [jax.ShapeDtypeStruct((pairs, BLOCK, local_blocks * rank), f32)] * 2
            out_specs = [VMEM] * 2
        else:
            outs, out_specs = jax.ShapeDtypeStruct((pairs, tall, wide), f32), VMEM
        return call(
            functools.partial(
                low_kernel, group, layers, rows, chunks, depth, rank, tuple(at), len(taken), by_request,
                shift, before is not None, last,
            ),
            outs,
            out_specs,
            [SMEM] * 3 + [HBM] * (len(tokens_here) + len(taken)) + [VMEM] * (before is not None),
            [pltpu.VMEM((group * rows, len(at) * depth), bf16)]
            + [pltpu.VMEM(v.shape, bf16) for v in taken]
            + [pltpu.SemaphoreType.DMA((len(tokens_here), len(at))), pltpu.SemaphoreType.DMA((len(taken),))],
            WAITS["low"][last] * CORE_FLOPS_PER_US,
            0,
        )(*lists, *tokens_here, *taken, *([before] if before is not None else []))

    early = low_call([([0], down)] + down_bundles[:-1], None, False)
    even, odd = low_call(down_bundles[-1:], early, True)
    got = swap(odd, "batch", 1)
    lows = layer_pairs(even, got)

    return call(
        functools.partial(final_kernel, rows, rank, len(bases), len(fars), len(lows)),
        jax.ShapeDtypeStruct((rows, out_width), bf16),
        VMEM,
        [SMEM] * 3 + [VMEM] * (len(fars) + len(bases) + len(lows)) + [HBM],
        [pltpu.VMEM((local_blocks, rank, out_width), bf16), pltpu.SemaphoreType.DMA((local_blocks,))],
        2 * rows * rank * out_width,
        8 * rows * out_width,
    )(*lists, *fars, *bases, *lows, adapter_up_factors)


def layer_pairs(mine, got):
    bit = 2
    while mine.shape[0] > 1:
        total = mine + got
        mine, got = total[0::2], swap(total[1::2], "batch", bit)
        bit *= 2
    return [mine[0], got[0]]


def solution(mesh):
    placed = (
        P(("rep", "batch"), None),
        P("batch", None),
        P("batch", None, None),
        P(),
        P("rep"),
        P("rep"),
        P("rep"),
    )
    return jax.shard_map(
        shards, mesh=mesh, in_specs=placed, out_specs=P(("rep", "batch"), None), check_vma=False
    )
```

```python
import functools

import jax
import jax.numpy as jnp
from jax import lax
from jax.experimental import pallas as pl
from jax.experimental.pallas import tpu as pltpu
from jax.sharding import PartitionSpec as P

BLOCK = 128
LANES = 128
MOST = 16
LAYER_CHIPS = 4
VMEM_BYTES = 28 * 1024 * 1024
CORE_FLOPS_PER_US = 1_153_500_000
CFG = {'us': {'all': 30, 'far': 12}, 'z3': 2, 'c': 'W', 'xcut': 2, 'ph': [13, 3]}
WAITS = {"far": 12, "keys": 0, "all": 5, "across": 0, "near": 0, "low": (5, 15)}
WAITS.update(CFG.get("us", {}))
PHASES = tuple(CFG.get("ph", [8, 8]))

HBM = pl.BlockSpec(memory_space=pl.ANY)
VMEM = pl.BlockSpec(memory_space=pltpu.VMEM)
SMEM = pl.BlockSpec(memory_space=pltpu.SMEM)


def call(kernel, outs, out_specs, in_specs, scratch, flops, moved):
    return pl.pallas_call(
        kernel,
        out_shape=outs,
        in_specs=in_specs,
        out_specs=out_specs,
        scratch_shapes=scratch,
        compiler_params=pltpu.CompilerParams(vmem_limit_bytes=VMEM_BYTES),
        cost_estimate=pl.CostEstimate(flops=flops, bytes_accessed=moved, transcendentals=0),
    )


def swap(value, axis, bit):
    return lax.ppermute(value, axis, [(i, i ^ bit) for i in range(lax.axis_size(axis))])


def run_copies(pairs, sems):
    copies = [pltpu.make_async_copy(a, b, sems.at[i]) for i, (a, b) in enumerate(pairs)]
    for copy in copies:
        copy.start()
    return copies


def part_start(h, part):
    return pl.multiple_of((lax.axis_index("rep") ^ h) * part, part)


def first_kernel(group, layers, splits, part, chunks, key, tokens, *refs):
    keys, refs = refs[:splits], refs[splits:]
    outs, sems = refs[:-1], refs[-1]
    depth = splits * part
    me = lax.axis_index("batch")
    layer, spot = me // group, me % group
    pairs = [(key.at[pl.ds(part_start(h, part), part), :], keys[h]) for h in range(splits)]
    for s in reversed(range(group)):
        for t in range(layers):
            first = ((layer ^ t) * group + (spot ^ s)) * depth
            for h in range(splits):
                start = first + part_start(h, part) if splits > 1 else first
                start = pl.multiple_of(start, part)
                to = pl.ds(t * depth + h * part, part)
                if s < 2:
                    pairs.append((tokens.at[:, pl.ds(start, part)], outs[s].at[:, to]))
                    continue
                for j, (row, deep) in enumerate(chunks):
                    pairs.append(
                        (
                            tokens.at[pl.ds(row, deep), pl.ds(start, part)],
                            outs[2 + (s - 2) * len(chunks) + j].at[:, to],
                        )
                    )
    for copy in run_copies(pairs, sems):
        copy.wait()


def stack_kernel(moves, taken, count, *refs):
    values, outs, sems = refs[:taken], refs[count:-1], refs[-1]
    pairs = []
    for o, to, a, row, rows in moves:
        pairs.append((values[a].at[pl.ds(row, rows), :], outs[o].at[pl.ds(to, rows), :]))
    for copy in run_copies(pairs, sems):
        copy.wait()


def stack(lists, *ready, us=0):
    values, moves, outs = [], [], []
    for o, rows_of in enumerate(lists):
        to = 0
        for value, row, rows in rows_of:
            moves.append((o, to, len(values), row, rows))
            values.append(value)
            to += rows
        outs.append(jax.ShapeDtypeStruct((to, value.shape[1]), value.dtype))
    count = len(values) + len(ready)
    return call(
        functools.partial(stack_kernel, tuple(moves), len(values), count),
        outs,
        [VMEM] * len(outs),
        [HBM] * count,
        [pltpu.SemaphoreType.DMA((len(moves),))],
        us * CORE_FLOPS_PER_US,
        0,
    )(*values, *ready)


def gate(value, *ready, us=0):
    return stack([[(value, 0, value.shape[0])]], *ready, us=us)[0]


def chosen_kernel(slots, rank, splits, part, group, layers, shift, picks, down, *refs):
    outs, sems = refs[:-1], refs[-1]
    layer = lax.axis_index("batch") // group
    half = (layer * 2) // layers
    pairs = []
    for n, out in enumerate(outs):
        first = (half ^ 1 ^ n) * shift
        for q in range(slots):
            for h in range(splits):
                start = part_start(h, part) if splits > 1 else 0
                pairs.append(
                    (
                        down.at[picks[first + q], :, pl.ds(start, part)],
                        out.at[pl.ds(q * rank, rank), pl.ds(h * part, part)],
                    )
                )
    for copy in run_copies(pairs, sems):
        copy.wait()


def table(lists, block):
    sizes, adapters, tails = lists
    end = jnp.int32(0)
    owner, adapter, limit = jnp.int32(0), jnp.int32(0), jnp.int32(BLOCK)
    for q in range(sizes.shape[0]):
        begin = end
        end = end + sizes[q]
        inside = (begin <= block) & (block < end)
        owner = jnp.where(inside, q, owner)
        adapter = jnp.where(inside, adapters[q], adapter)
        limit = jnp.where(inside & (block == end - 1), tails[q], limit)
    return owner, adapter, limit


def token_places(group, rows, chunks):
    near = [(s * rows, rows) for s in range(min(group, 2))]
    far = [(s * rows + row, deep) for s in range(2, group) for row, deep in chunks]
    return near + far


def low_kernel(
    group, layers, rows, chunks, depth, rank, entries, count, by_request, shift, has_sum, last, *refs
):
    lists, refs = refs[:3], refs[3:]
    places = token_places(group, rows, chunks)
    toks, refs = refs[: len(places)], refs[len(places) :]
    arrays, refs = refs[:count], refs[count:]
    if has_sum:
        before, refs = refs[0], refs[1:]
    if last:
        even, odd, refs = refs[0], refs[1], refs[2:]
    else:
        after, refs = refs[0], refs[1:]
    local_blocks = rows // BLOCK
    me = lax.axis_index("batch")
    layer, spot = me // group, me % group
    slots = []
    for s in range(group):
        for j in range(local_blocks):
            block = (layer * group + (spot ^ s)) * local_blocks + j
            owner, adapter, _ = table(lists, block)
            slots.append(owner - (layer * 2) // layers * shift if by_request else adapter)
    wide = 2 * local_blocks
    sums = [before[p] if has_sum else None for p in range(group // 2)]
    for n, (t, a, row) in enumerate(entries):
        for p in range(group // 2):
            chosen = jnp.concatenate(
                [
                    arrays[a][pl.ds(pl.multiple_of(row + slots[p * wide + i] * rank, rank), rank), :]
                    for i in range(wide)
                ],
                0,
            )
            held = jnp.concatenate(
                [
                    toks[i][:, t * depth : (t + 1) * depth]
                    for i, (to, _) in enumerate(places)
                    if to // (2 * rows) == p
                ],
                0,
            )
            term = lax.dot_general(
                held,
                chosen,
                (((1,), (1,)), ((), ())),
                preferred_element_type=jnp.float32,
            )
            sums[p] = term if sums[p] is None else sums[p] + term
    for p in range(group // 2):
        if not last:
            after[p] = sums[p]
            continue
        for out, at in ((even, 0), (odd, 1)):
            out[p] = jnp.concatenate(
                [
                    sums[p][
                        (at * local_blocks + j) * BLOCK : (at * local_blocks + j + 1) * BLOCK,
                        (at * local_blocks + j) * rank : (at * local_blocks + j + 1) * rank,
                    ]
                    for j in range(local_blocks)
                ],
                1,
            )


def final_kernel(rows, rank, bases, fars, lows, *refs):
    lists, refs = refs[:3], refs[3:]
    far_refs, refs = refs[:fars], refs[fars:]
    base_refs, refs = refs[:bases], refs[bases:]
    low_refs, refs = refs[:lows], refs[lows:]
    ups, out, up_here, sems = refs
    local_blocks = rows // BLOCK
    me = lax.axis_index("batch")
    found = [table(lists, me * local_blocks + j) for j in range(local_blocks)]
    copies = run_copies([(ups.at[found[j][1]], up_here.at[j]) for j in range(local_blocks)], sems)
    low = low_refs[0][...]
    for ref in low_refs[1:]:
        low = low + ref[...]
    low = low.astype(jnp.bfloat16)
    for j in range(local_blocks):
        copies[j].wait()
        here = pl.ds(j * BLOCK, BLOCK)
        total = jnp.dot(
            low[:, j * rank : (j + 1) * rank], up_here[j], preferred_element_type=jnp.float32
        )
        for ref in base_refs:
            total = total + ref[here, :]
        if far_refs:
            total = total + far_refs[0][here, :].astype(jnp.float32)
        live = lax.broadcasted_iota(jnp.int32, total.shape, 0) < found[j][2]
        out[here, :] = jnp.where(live, total, 0.0).astype(jnp.bfloat16)


def shards(
    tokens,
    key_matrix,
    adapter_down_factors,
    adapter_up_factors,
    request_block_list,
    request_adapter_index,
    request_tail_tokens,
):
    rows, width = tokens.shape
    depth, out_width = key_matrix.shape
    adapters, rank = adapter_down_factors.shape[1:]
    reps, devices = lax.axis_size("rep"), lax.axis_size("batch")
    group = 2 * LAYER_CHIPS // reps
    layers = devices // group
    splits = reps if (depth // reps) % LANES == 0 else 1
    part = depth // splits
    local_blocks = rows // BLOCK
    held_width = layers * depth
    lists = (request_block_list, request_adapter_index, request_tail_tokens)
    f32, bf16 = jnp.float32, jnp.bfloat16

    chunks = [
        (sum(PHASES[:i]) * rows // sum(PHASES), PHASES[i] * rows // sum(PHASES))
        for i in range(len(PHASES) if group > 2 else 0)
    ]
    far_count = (group - 2) * len(chunks)
    first = call(
        functools.partial(first_kernel, group, layers, splits, part, chunks),
        [jax.ShapeDtypeStruct((part, out_width), bf16)] * splits
        + [jax.ShapeDtypeStruct((rows, held_width), bf16)] * 2
        + [jax.ShapeDtypeStruct((deep, held_width), bf16) for _, deep in chunks] * (group - 2),
        [HBM] * (splits + 2 + far_count),
        [HBM] * 2,
        [
            pltpu.SemaphoreType.DMA(
                (splits + (2 + far_count) * layers * splits,)
            )
        ],
        0,
        4 * (rows * width + depth * out_width),
    )(key_matrix, tokens)
    key_parts, first = first[:splits], first[splits:]

    far = [list(first[2 + s * len(chunks) :][: len(chunks)]) for s in range(group - 2)]
    sent = []
    for j, (_, deep) in enumerate(chunks):
        if j:
            sent = stack([[(f[j], 0, deep)] for f in far], *[f[j - 1] for f in far], us=WAITS["far"])
        else:
            sent = [f[j] for f in far]
        for s, f in enumerate(far):
            f[j] = swap(sent[s], "batch", 2 + s)

    down = jnp.transpose(adapter_down_factors, (1, 2, 0))
    requests = request_adapter_index.shape[0]
    by_request = requests < adapters
    shift = 1 if by_request and local_blocks * devices == 2 * MOST and layers > 1 else 0
    slots = requests - shift if by_request else adapters
    if by_request:
        across, down = call(
            functools.partial(chosen_kernel, slots, rank, splits, part, group, layers, shift),
            [jax.ShapeDtypeStruct((slots * rank, depth), bf16)] * 2,
            [VMEM] * 2,
            [SMEM, HBM],
            [pltpu.SemaphoreType.DMA((2 * slots * splits,))],
            0,
            8 * slots * rank * depth,
        )(request_adapter_index, down)
    else:
        down = down.reshape(slots * rank, depth)
        across = down

    def over_layers(across, near):
        bundles = []
        bit = layers // 2
        while bit:
            moved = [([bit], swap(near if bundles else across, "batch", bit * group))]
            if bundles:
                rest = [v for _, v in bundles]
                rest = rest[0] if len(rest) == 1 else jnp.concatenate(rest, 0)
                order = [t ^ bit for ts, _ in bundles for t in ts]
                moved.append((order, swap(rest, "batch", bit * group)))
            bundles = bundles + moved
            bit //= 2
        return bundles

    key_bundles = over_layers(key_parts[0], key_parts[0])
    rows_of_key = {}
    for h in range(splits):
        rows_of_key[0, h] = (key_parts[h], 0, part)
    for ts, value in key_bundles:
        for i, t in enumerate(ts):
            rows_of_key[t, 0] = (value, i * part, part)
    last_keys = [key_bundles[-1][1]]
    xcut = CFG.get("xcut", 1)
    for h in range(1, splits):
        swapped = None
        for bundles in (key_bundles[:xcut], key_bundles[xcut:]):
            if not bundles:
                continue
            values = bundles[0][1]
            ready = [swapped] if swapped is not None and (len(bundles) > 1 or CFG.get("x3g")) else []
            if len(bundles) > 1 or ready:
                values = stack([[(v, 0, v.shape[0]) for _, v in bundles]], *ready, us=WAITS["keys"])[0]
            last_keys = [values]
            swapped = swap(values, "rep", h)
            for i, t in enumerate([t for ts, _ in bundles for t in ts]):
                rows_of_key[t, h] = (swapped, i * part, part)
    keys = stack(
        [[rows_of_key[t, h] for t in range(layers) for h in range(splits)]], us=WAITS["all"]
    )[0]

    across_sent = gate(across, *[v for _, v in key_bundles[:CFG.get('z3', 2)]], us=WAITS["across"])
    down_sent = gate(down, *last_keys, us=WAITS["near"])
    if CFG.get("zdirect") and layers == 4:
        d = {2: swap(across_sent, "batch", 2 * group)}
        sent3 = gate(across, *[{"k3": last_keys[0], "Z3": d[2], "gZ5": down_sent}[k] for k in CFG.get("z6", ["k3"])], us=WAITS.get("z6", 0))
        d[1] = swap(down_sent, "batch", group)
        d[3] = swap(sent3, "batch", 3 * group)
        down_bundles = [([t], d[t]) for t in (2, 1, 3)]
    else:
        down_bundles = over_layers(across_sent, down_sent)

    cm = CFG.get("c", 2)
    c_ready = {"W": [keys], "Z3W": [keys, down_bundles[0][1]], "X": [swapped] if splits > 1 else []}.get(cm) if isinstance(cm, str) else [v for _, v in down_bundles[:cm]]
    near = [first[0], swap(gate(first[1], *c_ready) if cm else first[1], "batch", 1)]

    def base_of(value):
        return jnp.dot(value, keys, preferred_element_type=f32)

    fars = []
    if far:
        sums = []
        for j in range(len(chunks)):
            theirs = swap(base_of(far[1][j]), "batch", 1)
            sums.append((base_of(far[0][j]) + theirs).astype(bf16))
        if CFG.get("ymerge"):
            sums = [jnp.concatenate(sums, 0)]
        if CFG.get("lowe"):
            down = gate(down, sums[0])
        fars = [swap(v, "batch", 2) for v in sums]
        if CFG.get("lowl"):
            order, value = down_bundles[-1]
            down_bundles[-1] = (order, gate(value, fars[0]))
        fars = [fars[0] if len(fars) == 1 else jnp.concatenate(fars, 0)]
    bases = [base_of(near[0]), swap(base_of(near[1]), "batch", 1)]
    tokens_here = near + [value for f in far for value in f]

    def low_call(bundles, before, last):
        taken = [value for _, value in bundles]
        at = [
            (t, a, i * slots * rank) for a, (ts, _) in enumerate(bundles) for i, t in enumerate(ts)
        ]
        pairs, tall, wide = group // 2, 2 * rows, 2 * local_blocks * rank
        if last:
            outs = [jax.ShapeDtypeStruct((pairs, BLOCK, local_blocks * rank), f32)] * 2
            out_specs = [VMEM] * 2
        else:
            outs, out_specs = jax.ShapeDtypeStruct((pairs, tall, wide), f32), VMEM
        return call(
            functools.partial(
                low_kernel, group, layers, rows, chunks, depth, rank, tuple(at), len(taken), by_request,
                shift, before is not None, last,
            ),
            outs,
            out_specs,
            [SMEM] * 3 + [VMEM] * (len(tokens_here) + len(taken) + (before is not None)),
            [],
            WAITS["low"][last] * CORE_FLOPS_PER_US,
            0,
        )(*lists, *tokens_here, *taken, *([before] if before is not None else []))

    early = low_call([([0], down)] + down_bundles[:-1], None, False)
    even, odd = low_call(down_bundles[-1:], early, True)
    got = swap(odd, "batch", 1)
    lows = layer_pairs(even, got)

    return call(
        functools.partial(final_kernel, rows, rank, len(bases), len(fars), len(lows)),
        jax.ShapeDtypeStruct((rows, out_width), bf16),
        VMEM,
        [SMEM] * 3 + [VMEM] * (len(fars) + len(bases) + len(lows)) + [HBM],
        [pltpu.VMEM((local_blocks, rank, out_width), bf16), pltpu.SemaphoreType.DMA((local_blocks,))],
        2 * rows * rank * out_width,
        8 * rows * out_width,
    )(*lists, *fars, *bases, *lows, adapter_up_factors)


def layer_pairs(mine, got):
    bit = 2
    while mine.shape[0] > 1:
        total = mine + got
        mine, got = total[0::2], swap(total[1::2], "batch", bit)
        bit *= 2
    return [mine[0], got[0]]


def solution(mesh):
    placed = (
        P(("rep", "batch"), None),
        P("batch", None),
        P("batch", None, None),
        P(),
        P("rep"),
        P("rep"),
        P("rep"),
    )
    return jax.shard_map(
        shards, mesh=mesh, in_specs=placed, out_specs=P(("rep", "batch"), None), check_vma=False
    )
```
